32 devices in a mesh: dp: 4 (over z), ctx: 8 (over y, x, core).
Axes of the slice: x: 2, y: 2, z: 4, core: 2. Of those that a mesh axis runs over, the one named last changes fastest.
Arguments:
- queries: bfloat16 [4, 1024, 2048], P('dp', 'ctx'), may hold values from -6 to 6
- keys: bfloat16 [4, 1024, 2048], P('dp', 'ctx'), may hold values from -6 to 6
- values: bfloat16 [4, 1024, 2048], P('dp', 'ctx'), may hold values from -6 to 6
- grad_output: bfloat16 [4, 1024, 2048], P('dp', 'ctx'), may hold values from -6 to 6
- out_gain: float32 [2048], replicated, may hold values from 0.5 to 1.5
- doc_lengths: int32 [4, 12], P('dp'), may hold values from 1 to 341, 1024 in all within a row
Outputs:
- output: bfloat16 [4, 1024, 2048], P('dp', 'ctx')
- grad_queries: bfloat16 [4, 1024, 2048], P('dp', 'ctx')
- grad_keys: bfloat16 [4, 1024, 2048], P('dp', 'ctx')
- grad_values: bfloat16 [4, 1024, 2048], P('dp', 'ctx')
- grad_gain: float32 [2048], replicated
The draws below stay inside these ranges and needn't reach their ends.
Inputs may be any that keep to these rules, and one draw needn't show every extreme that they name: `doc_lengths`: each row holds the lengths of 12 documents packed end to end; they sum to 1024, and the largest is exactly 341.
All inputs are finite; a program needn't handle non-finite values.
Results may differ from the reference program's by a relative error of at most 0.012.
The reference program's roundings to bfloat16 on the way count: a program that leaves them out, or rounds other values in their place, can miss the bound.
Values may be sent and summed in bfloat16 or wider, within the bound.
A program may use at most 64 MiB of HBM per device.

```python
import math
import jax
import jax.numpy as jnp
import numpy as np
from jax import lax

H = 32
E = 64
DOCS = 12
BATCH = 4
LEN = 1024
BLK = 128
HE = 2048


def shard_levels(rng, extent, cuts, low, largest):
    factor_of, own = 1.0, jax.random.fold_in(rng, 6)
    for dim, blocks in cuts:
        heights = jnp.exp(jax.random.uniform(jax.random.fold_in(own, dim), (blocks,), jnp.float32, low / len(cuts), largest / len(cuts)))
        factor_of = factor_of * jnp.repeat(heights, extent[dim] // blocks).reshape([-1 if axis == dim else 1 for axis in range(len(extent))])
    return factor_of


def profile(number_of, total, reach, slope):
    loads = [(1 << 20) // math.isqrt(rank ** slope) + 1 for rank in range(2, number_of + 1)]
    surplus, given = total - reach - (number_of - 1), [1] * (number_of - 1)
    while surplus > 0:
        candidates = [i for i in range(number_of - 1) if given[i] < reach]
        whole, budget = sum([loads[i] for i in candidates]), surplus
        for i in candidates:
            extra = min(reach - given[i], max(1, budget * loads[i] // whole), surplus)
            given[i] = given[i] + extra
            surplus = surplus - extra
    return np.array([reach] + given)


def ragged(rng, count, total, most, lean):
    if count == 2:
        one = jax.random.randint(rng, (), max(1, total - most), min(most, total - 1) + 1)
        return jnp.stack([one, total - one])
    tallies = jnp.asarray(profile(count, total, most, lean), jnp.int32)
    pairs = (count - 1) // 2
    donor, sink = tallies[1:1 + 2 * pairs:2], tallies[2:2 + 2 * pairs:2]
    margin = jnp.minimum(donor - 1, most - sink)
    shifted = jax.random.randint(jax.random.fold_in(rng, 1), (pairs,), 0, 1 << 20) % (margin + 1)
    tallies = tallies.at[1:1 + 2 * pairs:2].set(donor - shifted).at[2:2 + 2 * pairs:2].set(sink + shifted)
    return tallies[jax.random.permutation(jax.random.fold_in(rng, 2), count)]


def bell_draw(rng, shape, width, bound, cuts=(), kind=jnp.bfloat16):
    level = shard_levels(rng, shape, cuts, -0.22, 0.18) if cuts else 1.0
    result = jax.random.normal(rng, shape, jnp.float32) * width * level
    return jnp.minimum(jnp.maximum(result, -bound), bound).astype(kind)


def setup_inputs(seed: int = 0) -> dict:
    splits = jax.random.split(jax.random.key(seed), 7)
    return {
        "queries": bell_draw(splits[0], (BATCH, LEN, HE), 1.0, 6.0, ((0, 4), (1, 8))),
        "keys": bell_draw(splits[1], (BATCH, LEN, HE), 1.0, 6.0, ((0, 4), (1, 8))),
        "values": bell_draw(splits[2], (BATCH, LEN, HE), 1.0, 6.0, ((0, 4), (1, 8))),
        "grad_output": bell_draw(splits[3], (BATCH, LEN, HE), 1.0, 6.0, ((0, 4), (1, 8))),
        "out_gain": jnp.clip(1.0 + 0.1 * jax.random.normal(splits[4], (HE,), jnp.float32), 0.5, 1.5),
        "doc_lengths": jax.vmap(lambda own: ragged(own, DOCS, LEN, LEN // 3, 2))(jax.random.split(splits[5], BATCH)).reshape((BATCH, DOCS)).astype(jnp.int32),
    }


eps = 1e-05
precise = lax.Precision.HIGHEST

def geometry(length_row):
    doc_ends = jnp.cumsum(length_row).astype(jnp.int32)
    begins = (doc_ends - length_row).astype(jnp.int32)
    positions = jnp.arange(LEN, dtype=jnp.int32)
    doc_ids = lax.optimization_barrier(jnp.sum((positions[:, None] >= doc_ends[None, :]).astype(jnp.int32), axis=1)).astype(jnp.int32)
    starts = lax.optimization_barrier(jnp.sum((positions[:, None] == begins[None, :]).astype(jnp.float32), axis=1))
    return (doc_ids, starts)

def chain_step(carried, pieces):
    state_piece, open_piece = pieces
    return (state_piece + (1.0 - open_piece) * carried, carried)

def reference(queries, keys, values, grad_output, out_gain, doc_lengths):
    nblocks = LEN // BLK
    gain_heads = out_gain.reshape(H, E)

    def one_sequence(packed):
        qs, ks, vs, gs, length_row = packed
        doc_ids, starts = geometry(length_row)
        doc_ids = doc_ids.reshape(nblocks, BLK)
        starts = starts.reshape(nblocks, BLK)
        shape4 = (nblocks, BLK, H, E)
        qf = qs.reshape(shape4).astype(jnp.float32)
        kf = ks.reshape(shape4).astype(jnp.float32)
        vf = vs.reshape(shape4).astype(jnp.float32)
        dyf = gs.reshape(shape4).astype(jnp.float32)
        counted = jnp.cumsum(starts, axis=1)
        totals = counted[:, -1:]
        before = (counted == 0).astype(jnp.float32)[:, :, None, None]
        after_mask = (totals - counted == 0).astype(jnp.float32)[:, :, None, None]
        opened = jnp.minimum(totals[:, 0], 1.0)
        row_ids = jnp.arange(BLK)
        causal = row_ids[:, None] >= row_ids[None, :]
        doc_mask = jnp.logical_and(causal[None], doc_ids[:, :, None] == doc_ids[:, None, :]).astype(jnp.float32)[:, None]
        scores = jnp.einsum('btge,bsge->bgts', qf, kf, precision=precise) * doc_mask
        weights = lax.optimization_barrier(scores.astype(jnp.bfloat16)).astype(jnp.float32)
        own_state = jnp.einsum('bsge,bsgf->bgef', kf * after_mask, vf, precision=precise)
        zero_state = jnp.zeros((H, E, E), jnp.float32)
        _, carried = lax.scan(chain_step, zero_state, (own_state, opened))
        attended = jnp.einsum('bgts,bsgf->btgf', weights, vf, precision=precise)
        attended = attended + before * jnp.einsum('btge,bgef->btgf', qf, carried, precision=precise)
        root_mean = jnp.sqrt(lax.optimization_barrier(jnp.mean(attended * attended, axis=-1, keepdims=True)) + eps)
        normed = attended / root_mean
        output = (gain_heads * normed).astype(jnp.bfloat16)
        dnormed = dyf * gain_heads
        grad_att = (dnormed - normed * lax.optimization_barrier(jnp.mean(dnormed * normed, axis=-1, keepdims=True))) / root_mean
        grad_att = lax.optimization_barrier(grad_att.astype(jnp.bfloat16)).astype(jnp.float32)
        gain_part = lax.optimization_barrier(jnp.sum(dyf * normed, axis=(0, 1)))
        grad_scores = jnp.einsum('btgf,bsgf->bgts', grad_att, vf, precision=precise) * doc_mask
        grad_weights = lax.optimization_barrier(grad_scores.astype(jnp.bfloat16)).astype(jnp.float32)
        back_state = jnp.einsum('btge,btgf->bgef', qf * before, grad_att, precision=precise)
        _, back_carried = lax.scan(chain_step, zero_state, (back_state, opened), reverse=True)
        grad_q = jnp.einsum('bgts,bsge->btge', grad_weights, kf, precision=precise)
        grad_q = grad_q + before * jnp.einsum('btgf,bgef->btge', grad_att, carried, precision=precise)
        grad_k = jnp.einsum('bgts,btge->bsge', grad_weights, qf, precision=precise)
        grad_k = grad_k + after_mask * jnp.einsum('bsgf,bgef->bsge', vf, back_carried, precision=precise)
        grad_v = jnp.einsum('bgts,btgf->bsgf', weights, grad_att, precision=precise)
        grad_v = grad_v + after_mask * jnp.einsum('bsge,bgef->bsgf', kf, back_carried, precision=precise)
        flat = (LEN, H * E)
        return (output.reshape(flat), grad_q.astype(jnp.bfloat16).reshape(flat), grad_k.astype(jnp.bfloat16).reshape(flat), grad_v.astype(jnp.bfloat16).reshape(flat), gain_part)
    outs = lax.map(one_sequence, (queries, keys, values, grad_output, doc_lengths))
    grad_gain = lax.optimization_barrier(jnp.sum(outs[4], axis=0)).reshape(H * E) / math.sqrt(BATCH * LEN)
    return (outs[0], outs[1], outs[2], outs[3], grad_gain)
```

```python
import functools
import math

import jax
import jax.numpy as jnp
from jax import lax
from jax.experimental import pallas as pl
from jax.experimental.pallas import tpu as pltpu
from jax.sharding import PartitionSpec as P

H = 32
E = 64
LANES = 2 * E
PAIRS = H // 2
CHUNKS = 4
PER = PAIRS // CHUNKS
EPS = 1e-05
BF = jnp.bfloat16
F32 = jnp.float32


def nn(a, b):
    return lax.dot_general(a, b, (((1,), (0,)), ((), ())), preferred_element_type=F32)


def nt(a, b):
    return lax.dot_general(a, b, (((1,), (1,)), ((), ())), preferred_element_type=F32)


def tn(a, b):
    return lax.dot_general(a, b, (((0,), (0,)), ((), ())), preferred_element_type=F32)


def kernel(
    n_ctx, n_dp, reach, total_tokens,
    lengths_ref, q_ref, k_ref, v_ref, dy_ref, gain_ref,
    out_ref, gq_ref, gk_ref, gv_ref, gg_ref,
    masks, doc_mask, own, back, fbuf, bbuf, carried, weights, att_s, gatt_s, gk_s, gv_s,
    gain_ctx, gain_dp,
    fsend, frecv, bsend, brecv, gsend, grecv, hsend, hrecv,
):
    me = lax.axis_index("ctx")
    mydp = lax.axis_index("dp")
    T = q_ref.shape[1]

    barrier = pltpu.get_barrier_semaphore()
    for d in range(1, n_ctx):
        pl.semaphore_signal(barrier, inc=1, device_id={"ctx": lax.rem(me + d, n_ctx)})
    for d in range(1, n_dp):
        pl.semaphore_signal(barrier, inc=1, device_id={"dp": lax.rem(mydp + d, n_dp)})

    docs = lengths_ref.shape[1]
    offset = me * T
    first, last = jnp.int32(1 << 20), jnp.int32(-(1 << 20))
    hits_f = [jnp.int32(0)] * (reach + 1)
    hits_b = [jnp.int32(0)] * (reach + 1)
    row = lax.broadcasted_iota(jnp.int32, (T, T), 0)
    col = lax.broadcasted_iota(jnp.int32, (T, T), 1)
    id_row = jnp.zeros((T, T), jnp.int32)
    id_col = jnp.zeros((T, T), jnp.int32)
    begin = -offset
    for i in range(docs):
        first = jnp.where(begin >= 0, jnp.minimum(first, begin), first)
        last = jnp.where(begin < T, jnp.maximum(last, begin), last)
        for d in range(2, reach + 1):
            hits_f[d] += jnp.where((begin >= -(d - 1) * T) & (begin < 0), 1, 0)
            hits_b[d] += jnp.where((begin >= T) & (begin < d * T), 1, 0)
        id_row += (row >= begin).astype(jnp.int32)
        id_col += (col >= begin).astype(jnp.int32)
        begin = begin + lengths_ref[0, i]
    coef_f = [jnp.where(hits_f[d] == 0, 1.0, 0.0).astype(F32) for d in range(reach + 1)]
    coef_b = [jnp.where(hits_b[d] == 0, 1.0, 0.0).astype(F32) for d in range(reach + 1)]
    dm = jnp.where((row >= col) & (id_row == id_col), 1.0, 0.0).astype(BF)
    doc_mask[0:T] = dm
    doc_mask[T:2 * T] = dm
    trow = lax.broadcasted_iota(jnp.int32, (T, LANES), 0)
    lane = lax.broadcasted_iota(jnp.int32, (T, LANES), 1)
    masks[0] = jnp.where(lane < E, 1.0, 0.0).astype(BF)
    masks[1] = jnp.where(lane < E, 0.0, 1.0).astype(BF)
    masks[2] = jnp.where(trow < first, 1.0, 0.0).astype(BF)
    masks[3] = jnp.where(trow >= last, 1.0, 0.0).astype(BF)

    for d in range(1, reach + 1):
        @pl.when(me - d < 0)
        def _():
            fbuf[d - 1] = jnp.zeros(fbuf.shape[1:], BF)

        @pl.when(me + d >= n_ctx)
        def _():
            bbuf[d - 1] = jnp.zeros(bbuf.shape[1:], BF)

    def lanes(p):
        return pl.ds(pl.multiple_of(p * LANES, LANES), LANES)

    def compact(full):
        left = lax.broadcasted_iota(jnp.int32, (E, LANES), 1) < E
        return jnp.where(left, full[:E], full[E:]).astype(BF)

    def diag(c):
        return jnp.concatenate([c * masks[0, 0:E], c * masks[1, 0:E]], axis=0)

    def stack(x):
        return jnp.concatenate([x * masks[0], x * masks[1]], axis=0)

    def fcopy(d, c):
        part = pl.ds(c * PER, PER)
        return pltpu.make_async_remote_copy(
            src_ref=own.at[part], dst_ref=fbuf.at[d - 1, part],
            send_sem=fsend.at[d - 1, c], recv_sem=frecv.at[d - 1, c],
            device_id={"ctx": lax.rem(me + d, n_ctx)},
        )

    def bcopy(d, c):
        part = pl.ds(c * PER, PER)
        return pltpu.make_async_remote_copy(
            src_ref=back.at[part], dst_ref=bbuf.at[d - 1, part],
            send_sem=bsend.at[d - 1, c], recv_sem=brecv.at[d - 1, c],
            device_id={"ctx": lax.rem(me - d + n_ctx, n_ctx)},
        )

    def loop(lo, hi, body):
        def step(p, _):
            body(p)
            return 0
        lax.fori_loop(lo, hi, step, 0)

    def state_of(p):
        own[p] = compact(tn(k_ref[0, :, lanes(p)] * masks[3], v_ref[0, :, lanes(p)]))

    for c in range(CHUNKS):
        loop(c * PER, (c + 1) * PER, state_of)
        if c == 0:
            pl.semaphore_wait(barrier, n_ctx + n_dp - 2)
        for d in range(1, reach + 1):
            @pl.when(me + d < n_ctx)
            def _():
                fcopy(d, c).start()

    def inside(p):
        q, k, v = q_ref[0, :, lanes(p)], k_ref[0, :, lanes(p)], v_ref[0, :, lanes(p)]
        w = nt(stack(q), k).astype(BF) * doc_mask[...]
        weights[p] = w
        att_s[p] = nn(jnp.concatenate([w[:T], w[T:]], axis=1), stack(v))

    loop(0, PAIRS, inside)

    jrow = lax.broadcasted_iota(jnp.int32, (2 * LANES, LANES), 0)
    jlane = lax.broadcasted_iota(jnp.int32, (2 * LANES, LANES), 1)
    mean_of = jnp.where((lax.rem(jrow, LANES) < E) == (jlane < E), 1.0 / E, 0.0).astype(BF)

    def head_mean(x):
        high = x.astype(BF)
        low = (x - high.astype(F32)).astype(BF)
        return nn(jnp.concatenate([high, low], axis=1), mean_of)

    def normalize(p):
        c = fbuf[0, p].astype(F32) * coef_f[1]
        for d in range(2, reach + 1):
            c += fbuf[d - 1, p].astype(F32) * coef_f[d]
        c = c.astype(BF)
        carried[p] = c
        qb = q_ref[0, :, lanes(p)] * masks[2]
        att = att_s[p] + nn(qb, diag(c))
        inv = lax.rsqrt(head_mean(att * att) + EPS)
        normed = att * inv
        gain = gain_ref[:, lanes(p)]
        out_ref[0, :, lanes(p)] = (gain * normed).astype(BF)
        dy = dy_ref[0, :, lanes(p)].astype(F32)
        dn = dy * gain
        gatt = ((dn - normed * head_mean(dn * normed)) * inv).astype(BF)
        gatt_s[p] = gatt
        gain_ctx[me, pl.ds(p, 1)] = jnp.sum(dy * normed, axis=0, keepdims=True)
        back[p] = compact(tn(qb, gatt))

    for c in range(CHUNKS):
        for d in range(1, reach + 1):
            @pl.when(me - d >= 0)
            def _():
                fcopy(d, c).wait_recv()
        loop(c * PER, (c + 1) * PER, normalize)
        for d in range(1, reach + 1):
            @pl.when(me - d >= 0)
            def _():
                bcopy(d, c).start()

    def gcopy(d, slot):
        return pltpu.make_async_remote_copy(
            src_ref=gain_ctx.at[slot], dst_ref=gain_ctx.at[slot],
            send_sem=gsend.at[d - 1], recv_sem=grecv.at[d - 1],
            device_id={"ctx": lax.rem(me + d, n_ctx)},
        )

    def hcopy(d, slot):
        return pltpu.make_async_remote_copy(
            src_ref=gain_dp.at[slot], dst_ref=gain_dp.at[slot],
            send_sem=hsend.at[d - 1], recv_sem=hrecv.at[d - 1],
            device_id={"dp": lax.rem(mydp + d, n_dp)},
        )

    for d in range(1, n_ctx):
        gcopy(d, me).start()

    def gradients(p):
        q, k, v = q_ref[0, :, lanes(p)], k_ref[0, :, lanes(p)], v_ref[0, :, lanes(p)]
        gatt = gatt_s[p]
        gs = stack(gatt)
        gw = nt(gs, v).astype(BF) * doc_mask[...]
        gq = nn(jnp.concatenate([gw[:T], gw[T:]], axis=1), stack(k))
        gq += nt(gatt * masks[2], diag(carried[p]))
        gq_ref[0, :, lanes(p)] = gq.astype(BF)
        gk_s[p] = tn(gw, stack(q))
        gv_s[p] = tn(weights[p], gs)

    loop(0, PAIRS, gradients)

    for d in range(1, n_ctx):
        gcopy(d, lax.rem(me - d + n_ctx, n_ctx)).wait_recv()
    total = gain_ctx[0]
    for i in range(1, n_ctx):
        total += gain_ctx[i]
    gain_dp[mydp] = total
    for d in range(1, n_dp):
        hcopy(d, mydp).start()

    def finish(p):
        c = bbuf[0, p].astype(F32) * coef_b[1]
        for d in range(2, reach + 1):
            c += bbuf[d - 1, p].astype(F32) * coef_b[d]
        bd = diag(c.astype(BF))
        after = masks[3]
        gk_ref[0, :, lanes(p)] = (gk_s[p] + nt(v_ref[0, :, lanes(p)] * after, bd)).astype(BF)
        gv_ref[0, :, lanes(p)] = (gv_s[p] + nn(k_ref[0, :, lanes(p)] * after, bd)).astype(BF)

    for c in range(CHUNKS):
        for d in range(1, reach + 1):
            @pl.when(me + d < n_ctx)
            def _():
                bcopy(d, c).wait_recv()
        loop(c * PER, (c + 1) * PER, finish)

    for d in range(1, n_dp):
        hcopy(d, lax.rem(mydp - d + n_dp, n_dp)).wait_recv()
    total = gain_dp[0]
    for i in range(1, n_dp):
        total += gain_dp[i]
    gg_ref[...] = total * (1.0 / math.sqrt(total_tokens))

    for c in range(CHUNKS):
        for d in range(1, reach + 1):
            @pl.when(me + d < n_ctx)
            def _():
                fcopy(d, c).wait_send()

            @pl.when(me - d >= 0)
            def _():
                bcopy(d, c).wait_send()
    for d in range(1, n_ctx):
        gcopy(d, me).wait_send()
    for d in range(1, n_dp):
        hcopy(d, mydp).wait_send()


def per_device(queries, keys, values, grad_output, out_gain, doc_lengths):
    _, T, width = queries.shape
    n_ctx, n_dp = lax.axis_size("ctx"), lax.axis_size("dp")
    length = T * n_ctx
    longest = length // 3
    reach = min(n_ctx - 1, -(-(longest - 1) // T))
    vmem = pl.BlockSpec(memory_space=pltpu.VMEM)
    data = jax.ShapeDtypeStruct((1, T, width), BF)
    dma = pltpu.SemaphoreType.DMA
    out = pl.pallas_call(
        functools.partial(kernel, n_ctx, n_dp, reach, n_dp * length),
        out_shape=(data,) * 4 + (jax.ShapeDtypeStruct((PAIRS, LANES), F32),),
        in_specs=[pl.BlockSpec(memory_space=pltpu.SMEM)] + [vmem] * 5,
        out_specs=(vmem,) * 5,
        scratch_shapes=[
            pltpu.VMEM((4, T, LANES), BF),
            pltpu.VMEM((2 * T, T), BF),
            pltpu.VMEM((PAIRS, E, LANES), BF),
            pltpu.VMEM((PAIRS, E, LANES), BF),
            pltpu.VMEM((reach, PAIRS, E, LANES), BF),
            pltpu.VMEM((reach, PAIRS, E, LANES), BF),
            pltpu.VMEM((PAIRS, E, LANES), BF),
            pltpu.VMEM((PAIRS, 2 * T, T), BF),
            pltpu.VMEM((PAIRS, T, LANES), F32),
            pltpu.VMEM((PAIRS, T, LANES), BF),
            pltpu.VMEM((PAIRS, T, LANES), F32),
            pltpu.VMEM((PAIRS, T, LANES), F32),
            pltpu.VMEM((n_ctx, PAIRS, LANES), F32),
            pltpu.VMEM((n_dp, PAIRS, LANES), F32),
            dma((reach, CHUNKS)), dma((reach, CHUNKS)),
            dma((reach, CHUNKS)), dma((reach, CHUNKS)),
            dma((n_ctx - 1,)), dma((n_ctx - 1,)),
            dma((n_dp - 1,)), dma((n_dp - 1,)),
        ],
        compiler_params=pltpu.CompilerParams(
            collective_id=0, has_side_effects=True, vmem_limit_bytes=48 * 1024 * 1024
        ),
    )(doc_lengths, queries, keys, values, grad_output, out_gain.reshape(1, width))
    return (*out[:4], out[4].reshape(width))


def solution(mesh):
    seq = P("dp", "ctx", None)
    return jax.shard_map(
        per_device,
        mesh=mesh,
        in_specs=(seq, seq, seq, seq, P(), P("dp", None)),
        out_specs=(seq, seq, seq, seq, P()),
        check_vma=False,
    )
```

```python
import functools
import math

import jax
import jax.numpy as jnp
from jax import lax
from jax.experimental import pallas as pl
from jax.experimental.pallas import tpu as pltpu
from jax.sharding import PartitionSpec as P

H = 32
E = 64
LANES = 2 * E
PAIRS = H // 2
CHUNKS = 4
PER = PAIRS // CHUNKS
EPS = 1e-05
VMEM_LIMIT = 58 * 1024 * 1024
BF = jnp.bfloat16
F32 = jnp.float32


def nn(a, b):
    return lax.dot_general(a, b, (((1,), (0,)), ((), ())), preferred_element_type=F32)


def nt(a, b):
    return lax.dot_general(a, b, (((1,), (1,)), ((), ())), preferred_element_type=F32)


def tn(a, b):
    return lax.dot_general(a, b, (((0,), (0,)), ((), ())), preferred_element_type=F32)


def kernel(
    n_ctx, n_dp, reach, total_tokens,
    lengths_hbm, q_hbm, k_hbm, v_hbm, dy_hbm, gain_hbm,
    out_hbm, gq_hbm, gk_hbm, gv_hbm, gg_hbm,
    lengths_ref, q_ref, k_ref, v_ref, dy_ref, gain_ref, in_sem, small_sem,
    out_ref, gq_ref, gk_ref, gv_ref, gg_ref, out_sem, gg_sem,
    masks, doc_mask, own, back, fbuf, bbuf, carried, weights, att_s, gatt_s, gk_s, gv_s,
    gain_ctx, gain_dp,
    fsend, frecv, bsend, brecv, gsend, grecv, hsend, hrecv,
):
    me = lax.axis_index("ctx")
    mydp = lax.axis_index("dp")
    T = q_ref.shape[1]

    small = [
        pltpu.make_async_copy(lengths_hbm, lengths_ref, small_sem.at[0]),
        pltpu.make_async_copy(gain_hbm, gain_ref, small_sem.at[1]),
    ]

    def incopy(i, c):
        source, target = ((k_hbm, k_ref), (v_hbm, v_ref), (q_hbm, q_ref), (dy_hbm, dy_ref))[i]
        part = pl.ds(pl.multiple_of(c * (PER * LANES), PER * LANES), PER * LANES)
        return pltpu.make_async_copy(
            source.at[:, :, part], target.at[:, :, part], in_sem.at[i, c]
        )

    def outcopy(i, c):
        source, target = (
            (out_ref, out_hbm), (gq_ref, gq_hbm), (gk_ref, gk_hbm), (gv_ref, gv_hbm)
        )[i]
        part = pl.ds(pl.multiple_of(c * (PER * LANES), PER * LANES), PER * LANES)
        return pltpu.make_async_copy(
            source.at[:, :, part], target.at[:, :, part], out_sem.at[i, c]
        )

    small[0].start()
    for c in range(CHUNKS):
        incopy(0, c).start()
        incopy(1, c).start()
    for c in range(CHUNKS):
        incopy(2, c).start()
    small[1].start()
    for c in range(CHUNKS):
        incopy(3, c).start()

    barrier = pltpu.get_barrier_semaphore()
    for d in range(1, n_ctx):
        pl.semaphore_signal(barrier, inc=1, device_id={"ctx": lax.rem(me + d, n_ctx)})
    for d in range(1, n_dp):
        pl.semaphore_signal(barrier, inc=1, device_id={"dp": lax.rem(mydp + d, n_dp)})

    small[0].wait()
    docs = lengths_ref.shape[1]
    offset = me * T
    first, last = jnp.int32(1 << 20), jnp.int32(-(1 << 20))
    hits_f = [jnp.int32(0)] * (reach + 1)
    hits_b = [jnp.int32(0)] * (reach + 1)
    row = lax.broadcasted_iota(jnp.int32, (T, T), 0)
    col = lax.broadcasted_iota(jnp.int32, (T, T), 1)
    id_row = jnp.zeros((T, T), jnp.int32)
    id_col = jnp.zeros((T, T), jnp.int32)
    begin = -offset
    for i in range(docs):
        first = jnp.where(begin >= 0, jnp.minimum(first, begin), first)
        last = jnp.where(begin < T, jnp.maximum(last, begin), last)
        for d in range(2, reach + 1):
            hits_f[d] += jnp.where((begin >= -(d - 1) * T) & (begin < 0), 1, 0)
            hits_b[d] += jnp.where((begin >= T) & (begin < d * T), 1, 0)
        id_row += (row >= begin).astype(jnp.int32)
        id_col += (col >= begin).astype(jnp.int32)
        begin = begin + lengths_ref[0, i]
    coef_f = [jnp.where(hits_f[d] == 0, 1.0, 0.0).astype(F32) for d in range(reach + 1)]
    coef_b = [jnp.where(hits_b[d] == 0, 1.0, 0.0).astype(F32) for d in range(reach + 1)]
    dm = jnp.where((row >= col) & (id_row == id_col), 1.0, 0.0).astype(BF)
    doc_mask[0:T] = dm
    doc_mask[T:2 * T] = dm
    trow = lax.broadcasted_iota(jnp.int32, (T, LANES), 0)
    lane = lax.broadcasted_iota(jnp.int32, (T, LANES), 1)
    masks[0] = jnp.where(lane < E, 1.0, 0.0).astype(BF)
    masks[1] = jnp.where(lane < E, 0.0, 1.0).astype(BF)
    masks[2] = jnp.where(trow < first, 1.0, 0.0).astype(BF)
    masks[3] = jnp.where(trow >= last, 1.0, 0.0).astype(BF)

    for d in range(1, reach + 1):
        @pl.when(me - d < 0)
        def _():
            fbuf[d - 1] = jnp.zeros(fbuf.shape[1:], BF)

        @pl.when(me + d >= n_ctx)
        def _():
            bbuf[d - 1] = jnp.zeros(bbuf.shape[1:], BF)

    def lanes(p):
        return pl.ds(pl.multiple_of(p * LANES, LANES), LANES)

    def compact(full):
        left = lax.broadcasted_iota(jnp.int32, (E, LANES), 1) < E
        return jnp.where(left, full[:E], full[E:]).astype(BF)

    def diag(c):
        return jnp.concatenate([c * masks[0, 0:E], c * masks[1, 0:E]], axis=0)

    def stack(x):
        return jnp.concatenate([x * masks[0], x * masks[1]], axis=0)

    def fcopy(d, c):
        part = pl.ds(c * PER, PER)
        return pltpu.make_async_remote_copy(
            src_ref=own.at[part], dst_ref=fbuf.at[d - 1, part],
            send_sem=fsend.at[d - 1, c], recv_sem=frecv.at[d - 1, c],
            device_id={"ctx": lax.rem(me + d, n_ctx)},
        )

    def bcopy(d, c):
        part = pl.ds(c * PER, PER)
        return pltpu.make_async_remote_copy(
            src_ref=back.at[part], dst_ref=bbuf.at[d - 1, part],
            send_sem=bsend.at[d - 1, c], recv_sem=brecv.at[d - 1, c],
            device_id={"ctx": lax.rem(me - d + n_ctx, n_ctx)},
        )

    def each(f, *lists):
        return [f(*items) for items in zip(*lists)]

    def chunk_loop(body):
        def step(c, _):
            body(c)
            return 0
        lax.fori_loop(0, CHUNKS, step, 0)

    def groups(c, size):
        return [[c * PER + g + i for i in range(size)] for g in range(0, PER, size)]

    def states(c):
        incopy(0, c).wait()
        incopy(1, c).wait()
        for ps in groups(c, 4):
            ks = [k_ref[0, :, lanes(p)] * masks[3] for p in ps]
            full = [tn(k, v_ref[0, :, lanes(p)]) for k, p in zip(ks, ps)]
            for p, x in zip(ps, full):
                own[p] = compact(x)

        @pl.when(c == 0)
        def _():
            pl.semaphore_wait(barrier, n_ctx + n_dp - 2)

        for d in range(1, reach + 1):
            @pl.when(me + d < n_ctx)
            def _():
                fcopy(d, c).start()

    chunk_loop(states)

    def inside(c):
        incopy(2, c).wait()
        for ps in groups(c, 2):
            qs = [stack(q_ref[0, :, lanes(p)]) for p in ps]
            scores = [nt(q, k_ref[0, :, lanes(p)]) for q, p in zip(qs, ps)]
            ws = [x.astype(BF) * doc_mask[...] for x in scores]
            for p, w in zip(ps, ws):
                weights[p] = w
            atts = [
                nn(jnp.concatenate([w[:T], w[T:]], axis=1), stack(v_ref[0, :, lanes(p)]))
                for w, p in zip(ws, ps)
            ]
            for p, att in zip(ps, atts):
                att_s[p] = att

    chunk_loop(inside)

    jrow = lax.broadcasted_iota(jnp.int32, (2 * LANES, LANES), 0)
    jlane = lax.broadcasted_iota(jnp.int32, (2 * LANES, LANES), 1)
    mean_of = jnp.where((lax.rem(jrow, LANES) < E) == (jlane < E), 1.0 / E, 0.0).astype(BF)

    def head_mean(x):
        high = x.astype(BF)
        low = (x - high.astype(F32)).astype(BF)
        return nn(jnp.concatenate([high, low], axis=1), mean_of)

    def gather(buf, coef, p):
        c = buf[0, p].astype(F32) * coef[1]
        for d in range(2, reach + 1):
            c += buf[d - 1, p].astype(F32) * coef[d]
        return c.astype(BF)

    small[1].wait()

    def normalize(c):
        for d in range(1, reach + 1):
            @pl.when(me - d >= 0)
            def _():
                fcopy(d, c).wait_recv()
        incopy(3, c).wait()
        for ps in groups(c, 4):
            cs = [gather(fbuf, coef_f, p) for p in ps]
            for p, x in zip(ps, cs):
                carried[p] = x
            qbs = [q_ref[0, :, lanes(p)] * masks[2] for p in ps]
            atts = [att_s[p] + nn(qb, diag(x)) for p, qb, x in zip(ps, qbs, cs)]
            means = [head_mean(att * att) for att in atts]
            invs = [lax.rsqrt(m + EPS) for m in means]
            normeds = each(lambda att, inv: att * inv, atts, invs)
            gains = [gain_ref[:, lanes(p)] for p in ps]
            for p, gain, normed in zip(ps, gains, normeds):
                out_ref[0, :, lanes(p)] = (gain * normed).astype(BF)
            dys = [dy_ref[0, :, lanes(p)].astype(F32) for p in ps]
            terms = each(lambda dy, normed: dy * normed, dys, normeds)
            for p, term in zip(ps, terms):
                gain_ctx[me, pl.ds(p, 1)] = jnp.sum(term, axis=0, keepdims=True)
            means = each(lambda term, gain: head_mean(term * gain), terms, gains)
            gatts = [
                ((dy * gain - normed * m) * inv).astype(BF)
                for dy, gain, normed, m, inv in zip(dys, gains, normeds, means, invs)
            ]
            for p, gatt in zip(ps, gatts):
                gatt_s[p] = gatt
            full = each(tn, qbs, gatts)
            for p, x in zip(ps, full):
                back[p] = compact(x)
        for d in range(1, reach + 1):
            @pl.when(me - d >= 0)
            def _():
                bcopy(d, c).start()
        outcopy(0, c).start()

    chunk_loop(normalize)

    def gcopy(d, slot):
        return pltpu.make_async_remote_copy(
            src_ref=gain_ctx.at[slot], dst_ref=gain_ctx.at[slot],
            send_sem=gsend.at[d - 1], recv_sem=grecv.at[d - 1],
            device_id={"ctx": lax.rem(me + d, n_ctx)},
        )

    def hcopy(d, slot):
        return pltpu.make_async_remote_copy(
            src_ref=gain_dp.at[slot], dst_ref=gain_dp.at[slot],
            send_sem=hsend.at[d - 1], recv_sem=hrecv.at[d - 1],
            device_id={"dp": lax.rem(mydp + d, n_dp)},
        )

    for d in range(1, n_ctx):
        gcopy(d, me).start()

    def gradients(c):
        for ps in groups(c, 2):
            gatts = [gatt_s[p] for p in ps]
            gss = each(stack, gatts)
            scores = [nt(gs, v_ref[0, :, lanes(p)]) for gs, p in zip(gss, ps)]
            for p, gs in zip(ps, gss):
                gv_s[p] = tn(weights[p], gs)
            gws = [x.astype(BF) * doc_mask[...] for x in scores]
            gqs = [
                nn(jnp.concatenate([gw[:T], gw[T:]], axis=1), stack(k_ref[0, :, lanes(p)]))
                + nt(gatt * masks[2], diag(carried[p]))
                for gw, gatt, p in zip(gws, gatts, ps)
            ]
            for p, gq in zip(ps, gqs):
                gq_ref[0, :, lanes(p)] = gq.astype(BF)
            for p, gw in zip(ps, gws):
                gk_s[p] = tn(gw, stack(q_ref[0, :, lanes(p)]))
        outcopy(1, c).start()

    chunk_loop(gradients)

    for d in range(1, n_ctx):
        gcopy(d, lax.rem(me - d + n_ctx, n_ctx)).wait_recv()
    total = gain_ctx[0]
    for i in range(1, n_ctx):
        total += gain_ctx[i]
    gain_dp[mydp] = total
    for d in range(1, n_dp):
        hcopy(d, mydp).start()

    def finish(c):
        for d in range(1, reach + 1):
            @pl.when(me + d < n_ctx)
            def _():
                bcopy(d, c).wait_recv()
        for ps in groups(c, 4):
            bds = [diag(gather(bbuf, coef_b, p)) for p in ps]
            after = masks[3]
            gks = [nt(v_ref[0, :, lanes(p)] * after, bd) for p, bd in zip(ps, bds)]
            gvs = [nn(k_ref[0, :, lanes(p)] * after, bd) for p, bd in zip(ps, bds)]
            for p, gk, gv in zip(ps, gks, gvs):
                gk_ref[0, :, lanes(p)] = (gk_s[p] + gk).astype(BF)
                gv_ref[0, :, lanes(p)] = (gv_s[p] + gv).astype(BF)
        outcopy(2, c).start()
        outcopy(3, c).start()

    chunk_loop(finish)

    for d in range(1, n_dp):
        hcopy(d, lax.rem(mydp - d + n_dp, n_dp)).wait_recv()
    total = gain_dp[0]
    for i in range(1, n_dp):
        total += gain_dp[i]
    gg_ref[...] = total * (1.0 / math.sqrt(total_tokens))
    gg_copy = pltpu.make_async_copy(gg_ref, gg_hbm, gg_sem)
    gg_copy.start()

    for c in range(CHUNKS):
        for d in range(1, reach + 1):
            @pl.when(me + d < n_ctx)
            def _():
                fcopy(d, c).wait_send()

            @pl.when(me - d >= 0)
            def _():
                bcopy(d, c).wait_send()
    for d in range(1, n_ctx):
        gcopy(d, me).wait_send()
    for d in range(1, n_dp):
        hcopy(d, mydp).wait_send()
    for i in range(4):
        for c in range(CHUNKS):
            outcopy(i, c).wait()
    gg_copy.wait()


def write_out(*refs):
    sources, targets, sems = refs[:5], refs[5:10], refs[10]
    copies = [
        pltpu.make_async_copy(source, target, sems.at[i])
        for i, (source, target) in enumerate(zip(sources, targets))
    ]
    for copy in copies:
        copy.start()
    for copy in copies:
        copy.wait()


def per_device(queries, keys, values, grad_output, out_gain, doc_lengths):
    _, T, width = queries.shape
    n_ctx, n_dp = lax.axis_size("ctx"), lax.axis_size("dp")
    length = T * n_ctx
    longest = length // 3
    reach = min(n_ctx - 1, -(-(longest - 1) // T))
    hbm = pl.BlockSpec(memory_space=pltpu.HBM)
    data = jax.ShapeDtypeStruct((1, T, width), BF)
    dma = pltpu.SemaphoreType.DMA
    shapes = (data,) * 4 + (jax.ShapeDtypeStruct((PAIRS, LANES), F32),)
    out = pl.pallas_call(
        functools.partial(kernel, n_ctx, n_dp, reach, n_dp * length),
        out_shape=shapes,
        in_specs=[hbm] * 6,
        out_specs=(hbm,) * 5,
        scratch_shapes=[
            pltpu.SMEM(doc_lengths.shape, jnp.int32),
            pltpu.VMEM((1, T, width), BF),
            pltpu.VMEM((1, T, width), BF),
            pltpu.VMEM((1, T, width), BF),
            pltpu.VMEM((1, T, width), BF),
            pltpu.VMEM((1, width), F32),
            dma((4, CHUNKS)),
            dma((2,)),
            pltpu.VMEM((1, T, width), BF),
            pltpu.VMEM((1, T, width), BF),
            pltpu.VMEM((1, T, width), BF),
            pltpu.VMEM((1, T, width), BF),
            pltpu.VMEM((PAIRS, LANES), F32),
            dma((4, CHUNKS)),
            dma,
            pltpu.VMEM((4, T, LANES), BF),
            pltpu.VMEM((2 * T, T), BF),
            pltpu.VMEM((PAIRS, E, LANES), BF),
            pltpu.VMEM((PAIRS, E, LANES), BF),
            pltpu.VMEM((reach, PAIRS, E, LANES), BF),
            pltpu.VMEM((reach, PAIRS, E, LANES), BF),
            pltpu.VMEM((PAIRS, E, LANES), BF),
            pltpu.VMEM((PAIRS, 2 * T, T), BF),
            pltpu.VMEM((PAIRS, T, LANES), F32),
            pltpu.VMEM((PAIRS, T, LANES), BF),
            pltpu.VMEM((PAIRS, T, LANES), F32),
            pltpu.VMEM((PAIRS, T, LANES), F32),
            pltpu.VMEM((n_ctx, PAIRS, LANES), F32),
            pltpu.VMEM((n_dp, PAIRS, LANES), F32),
            dma((reach, CHUNKS)), dma((reach, CHUNKS)),
            dma((reach, CHUNKS)), dma((reach, CHUNKS)),
            dma((n_ctx - 1,)), dma((n_ctx - 1,)),
            dma((n_dp - 1,)), dma((n_dp - 1,)),
        ],
        compiler_params=pltpu.CompilerParams(
            collective_id=0, has_side_effects=True, vmem_limit_bytes=VMEM_LIMIT
        ),
    )(doc_lengths, queries, keys, values, grad_output, out_gain.reshape(1, width))
    out = pl.pallas_call(
        write_out,
        out_shape=shapes,
        in_specs=[hbm] * 5,
        out_specs=(hbm,) * 5,
        scratch_shapes=[dma((5,))],
        compiler_params=pltpu.CompilerParams(vmem_limit_bytes=VMEM_LIMIT),
    )(*out)
    return (*out[:4], out[4].reshape(width))


def solution(mesh):
    seq = P("dp", "ctx", None)
    return jax.shard_map(
        per_device,
        mesh=mesh,
        in_specs=(seq, seq, seq, seq, P(), P("dp", None)),
        out_specs=(seq, seq, seq, seq, P()),
        check_vma=False,
    )
```

```python
import functools
import math

import jax
import jax.numpy as jnp
from jax import lax
from jax.experimental import pallas as pl
from jax.experimental.pallas import tpu as pltpu
from jax.sharding import PartitionSpec as P

H = 32
E = 64
LANES = 2 * E
PAIRS = H // 2
CHUNKS = 4
PER = PAIRS // CHUNKS
HALF = PER // 2
EPS = 1e-05
VMEM_LIMIT = 58 * 1024 * 1024
BF = jnp.bfloat16
F32 = jnp.float32


def nn(a, b):
    return lax.dot_general(a, b, (((1,), (0,)), ((), ())), preferred_element_type=F32)


def nt(a, b):
    return lax.dot_general(a, b, (((1,), (1,)), ((), ())), preferred_element_type=F32)


def tn(a, b):
    return lax.dot_general(a, b, (((0,), (0,)), ((), ())), preferred_element_type=F32)


def kernel(
    n_ctx, n_dp, reach, total_tokens,
    lengths_hbm, q_hbm, k_hbm, v_hbm, dy_hbm, gain_hbm,
    out_hbm, gq_hbm, gk_hbm, gv_hbm, gg_hbm,
    lengths_ref, q_ref, k_ref, v_ref, dy_ref, gain_ref, in_sem, small_sem,
    out_ref, gq_ref, gk_ref, gv_ref, gg_ref, out_sem, gg_sem,
    masks, doc_mask, own, back, fnear, bnear, fsum, bsum, fbuf, bbuf, fenter, benter, carried, weights, att_s, gatt_s, gk_s, gv_s,
    gain_ctx, gain_dp,
    fsems, bsems, gsend, grecv, hsend, hrecv,
):
    me = lax.axis_index("ctx")
    chip, side = me // 2, lax.rem(me, 2)
    partner = me + 1 - 2 * side
    n_chips = n_ctx // 2
    mydp = lax.axis_index("dp")
    T = q_ref.shape[1]

    small = [
        pltpu.make_async_copy(lengths_hbm, lengths_ref, small_sem.at[0]),
        pltpu.make_async_copy(gain_hbm, gain_ref, small_sem.at[1]),
    ]

    def incopy(i, c):
        source, target = ((k_hbm, k_ref), (v_hbm, v_ref), (q_hbm, q_ref), (dy_hbm, dy_ref))[i]
        part = pl.ds(pl.multiple_of(c * (PER * LANES), PER * LANES), PER * LANES)
        return pltpu.make_async_copy(
            source.at[:, :, part], target.at[:, :, part], in_sem.at[i, c]
        )

    def outcopy(i, c):
        source, target = (
            (out_ref, out_hbm), (gq_ref, gq_hbm), (gk_ref, gk_hbm), (gv_ref, gv_hbm)
        )[i]
        part = pl.ds(pl.multiple_of(c * (PER * LANES), PER * LANES), PER * LANES)
        return pltpu.make_async_copy(
            source.at[:, :, part], target.at[:, :, part], out_sem.at[i, c]
        )

    small[0].start()
    for c in range(CHUNKS):
        incopy(0, c).start()
        incopy(1, c).start()
    for c in range(CHUNKS):
        incopy(2, c).start()
    small[1].start()
    for c in range(CHUNKS):
        incopy(3, c).start()

    barrier = pltpu.get_barrier_semaphore()
    for d in range(1, n_ctx):
        pl.semaphore_signal(barrier, inc=1, device_id={"ctx": lax.rem(me + d, n_ctx)})
    for d in range(1, n_dp):
        pl.semaphore_signal(barrier, inc=1, device_id={"dp": lax.rem(mydp + d, n_dp)})

    small[0].wait()
    docs = lengths_ref.shape[1]
    offset = me * T
    first, last = jnp.int32(1 << 20), jnp.int32(-(1 << 20))
    hits_even, hits_odd = jnp.int32(0), jnp.int32(0)
    hits_f = [jnp.int32(0)] * (reach + 1)
    hits_b = [jnp.int32(0)] * (reach + 1)
    row = lax.broadcasted_iota(jnp.int32, (T, T), 0)
    col = lax.broadcasted_iota(jnp.int32, (T, T), 1)
    id_row = jnp.zeros((T, T), jnp.int32)
    id_col = jnp.zeros((T, T), jnp.int32)
    begin = -offset
    for i in range(docs):
        first = jnp.where(begin >= 0, jnp.minimum(first, begin), first)
        last = jnp.where(begin < T, jnp.maximum(last, begin), last)
        base = begin + side * T
        for d in range(2, reach + 1):
            hits_f[d] += jnp.where((base >= -(d - 1) * 2 * T) & (base < 0), 1, 0)
            hits_b[d] += jnp.where((base >= 2 * T) & (base < d * 2 * T), 1, 0)
        hits_even += jnp.where((base >= 0) & (base < T), 1, 0)
        hits_odd += jnp.where((base >= T) & (base < 2 * T), 1, 0)
        id_row += (row >= begin).astype(jnp.int32)
        id_col += (col >= begin).astype(jnp.int32)
        begin = begin + lengths_ref[0, i]
    coef_f = [jnp.where(hits_f[d] == 0, 1.0, 0.0).astype(F32) for d in range(reach + 1)]
    coef_b = [jnp.where(hits_b[d] == 0, 1.0, 0.0).astype(F32) for d in range(reach + 1)]
    keep_even = jnp.where(hits_even == 0, 1.0, 0.0).astype(F32)
    keep_odd = jnp.where(hits_odd == 0, 1.0, 0.0).astype(F32)
    odd = jnp.where(side == 1, 1.0, 0.0).astype(F32)
    sum_f = (odd + (1.0 - odd) * keep_odd, (1.0 - odd) + odd * keep_odd)
    sum_b = ((1.0 - odd) + odd * keep_even, odd + (1.0 - odd) * keep_even)
    enter_f = (odd, (1.0 - odd) + odd * keep_even)
    enter_b = (1.0 - odd, odd + (1.0 - odd) * keep_odd)
    dm = jnp.where((row >= col) & (id_row == id_col), 1.0, 0.0).astype(BF)
    doc_mask[0:T] = dm
    doc_mask[T:2 * T] = dm
    trow = lax.broadcasted_iota(jnp.int32, (T, LANES), 0)
    lane = lax.broadcasted_iota(jnp.int32, (T, LANES), 1)
    masks[0] = jnp.where(lane < E, 1.0, 0.0).astype(BF)
    masks[1] = jnp.where(lane < E, 0.0, 1.0).astype(BF)
    masks[2] = jnp.where(trow < first, 1.0, 0.0).astype(BF)
    masks[3] = jnp.where(trow >= last, 1.0, 0.0).astype(BF)

    for d in range(1, reach + 1):
        @pl.when(chip - d < 0)
        def _():
            fbuf[d - 1] = jnp.zeros(fbuf.shape[1:], BF)

        @pl.when(chip + d >= n_chips)
        def _():
            bbuf[d - 1] = jnp.zeros(bbuf.shape[1:], BF)

    def lanes(p):
        return pl.ds(pl.multiple_of(p * LANES, LANES), LANES)

    def compact(full):
        left = lax.broadcasted_iota(jnp.int32, (E, LANES), 1) < E
        return jnp.where(left, full[:E], full[E:]).astype(BF)

    def diag(c):
        return jnp.concatenate([c * masks[0, 0:E], c * masks[1, 0:E]], axis=0)

    def stack(x):
        return jnp.concatenate([x * masks[0], x * masks[1]], axis=0)

    def whole(c):
        return pl.ds(c * PER, PER)

    def mine(c):
        return pl.ds(c * PER + side * HALF, HALF)

    def links(state, near, summed, buf, enter, sems, sign):
        send, recv, far_send, far_recv, last_send, last_recv = sems

        def first_hop(c):
            return pltpu.make_async_remote_copy(
                src_ref=state.at[whole(c)], dst_ref=near.at[whole(c)],
                send_sem=send.at[c], recv_sem=recv.at[c], device_id={"ctx": partner},
            )

        def far_hop(d, c):
            return pltpu.make_async_remote_copy(
                src_ref=summed.at[mine(c)], dst_ref=buf.at[d - 1, mine(c)],
                send_sem=far_send.at[d - 1, c], recv_sem=far_recv.at[d - 1, c],
                device_id={"ctx": lax.rem(me + sign * 2 * d + n_ctx, n_ctx)},
            )

        def last_hop(c):
            return pltpu.make_async_remote_copy(
                src_ref=enter.at[mine(c)], dst_ref=enter.at[mine(c)],
                send_sem=last_send.at[c], recv_sem=last_recv.at[c],
                device_id={"ctx": partner},
            )

        def other_last_hop(c):
            theirs = pl.ds(c * PER + (1 - side) * HALF, HALF)
            return pltpu.make_async_remote_copy(
                src_ref=enter.at[theirs], dst_ref=enter.at[theirs],
                send_sem=last_send.at[c], recv_sem=last_recv.at[c],
                device_id={"ctx": partner},
            )

        def sends(d):
            return chip + d < n_chips if sign > 0 else chip - d >= 0

        def gets(d):
            return chip - d >= 0 if sign > 0 else chip + d < n_chips

        return first_hop, far_hop, last_hop, other_last_hop, sends, gets

    forward = links(own, fnear, fsum, fbuf, fenter, fsems, 1)
    backward = links(back, bnear, bsum, bbuf, benter, bsems, -1)

    def combine(c, link, state, near, summed, take):
        first_hop, far_hop, _, _, sends, _ = link
        first_hop(c).wait_recv()
        x = state[mine(c)].astype(F32) * take[0] + near[mine(c)].astype(F32) * take[1]
        summed[mine(c)] = x.astype(BF)
        for d in range(1, reach + 1):
            @pl.when(sends(d))
            def _():
                far_hop(d, c).start()

    def relay(c, link, buf, enter, coef):
        _, far_hop, last_hop, _, _, gets = link
        for d in range(1, reach + 1):
            @pl.when(gets(d))
            def _():
                far_hop(d, c).wait_recv()
        x = buf[0, mine(c)].astype(F32) * coef[1]
        for d in range(2, reach + 1):
            x += buf[d - 1, mine(c)].astype(F32) * coef[d]
        enter[mine(c)] = x.astype(BF)
        last_hop(c).start()

    def drain(link):
        first_hop, far_hop, last_hop, _, sends, _ = link
        for c in range(CHUNKS):
            first_hop(c).wait_send()
            last_hop(c).wait_send()
            for d in range(1, reach + 1):
                @pl.when(sends(d))
                def _():
                    far_hop(d, c).wait_send()

    def each(f, *lists):
        return [f(*items) for items in zip(*lists)]

    def chunk_loop(body, low=0, high=CHUNKS):
        def step(c, _):
            body(c)
            return 0
        lax.fori_loop(low, high, step, 0)

    def groups(c, size):
        return [[c * PER + g + i for i in range(size)] for g in range(0, PER, size)]

    def states(c):
        incopy(0, c).wait()
        incopy(1, c).wait()
        for ps in groups(c, 4):
            ks = [k_ref[0, :, lanes(p)] * masks[3] for p in ps]
            full = [tn(k, v_ref[0, :, lanes(p)]) for k, p in zip(ks, ps)]
            for p, x in zip(ps, full):
                own[p] = compact(x)

        @pl.when(c == 0)
        def _():
            pl.semaphore_wait(barrier, n_ctx + n_dp - 2)

        forward[0](c).start()

    chunk_loop(states)
    chunk_loop(lambda c: combine(c, forward, own, fnear, fsum, sum_f))

    def inside(c):
        incopy(2, c).wait()
        for ps in groups(c, 2):
            qs = [stack(q_ref[0, :, lanes(p)]) for p in ps]
            scores = [nt(q, k_ref[0, :, lanes(p)]) for q, p in zip(qs, ps)]
            ws = [x.astype(BF) * doc_mask[...] for x in scores]
            for p, w in zip(ps, ws):
                weights[p] = w
            atts = [
                nn(jnp.concatenate([w[:T], w[T:]], axis=1), stack(v_ref[0, :, lanes(p)]))
                for w, p in zip(ws, ps)
            ]
            for p, att in zip(ps, atts):
                att_s[p] = att

    def inside_and_relay(c):
        inside(c)
        for i in range(2):
            relay(2 * c - CHUNKS + i, forward, fbuf, fenter, coef_f)

    chunk_loop(inside, 0, CHUNKS // 2)
    chunk_loop(inside_and_relay, CHUNKS // 2)

    jrow = lax.broadcasted_iota(jnp.int32, (2 * LANES, LANES), 0)
    jlane = lax.broadcasted_iota(jnp.int32, (2 * LANES, LANES), 1)
    mean_of = jnp.where((lax.rem(jrow, LANES) < E) == (jlane < E), 1.0 / E, 0.0).astype(BF)

    def head_mean(x):
        high = x.astype(BF)
        low = (x - high.astype(F32)).astype(BF)
        return nn(jnp.concatenate([high, low], axis=1), mean_of)

    def gather(near, enter, take, p):
        return (near[p].astype(F32) * take[0] + enter[p].astype(F32) * take[1]).astype(BF)

    small[1].wait()

    def normalize(c):
        forward[3](c).wait_recv()
        incopy(3, c).wait()
        for ps in groups(c, 4):
            cs = [gather(fnear, fenter, enter_f, p) for p in ps]
            for p, x in zip(ps, cs):
                carried[p] = x
            qbs = [q_ref[0, :, lanes(p)] * masks[2] for p in ps]
            atts = [att_s[p] + nn(qb, diag(x)) for p, qb, x in zip(ps, qbs, cs)]
            means = [head_mean(att * att) for att in atts]
            invs = [lax.rsqrt(m + EPS) for m in means]
            normeds = each(lambda att, inv: att * inv, atts, invs)
            gains = [gain_ref[:, lanes(p)] for p in ps]
            for p, gain, normed in zip(ps, gains, normeds):
                out_ref[0, :, lanes(p)] = (gain * normed).astype(BF)
            dys = [dy_ref[0, :, lanes(p)].astype(F32) for p in ps]
            terms = each(lambda dy, normed: dy * normed, dys, normeds)
            for p, term in zip(ps, terms):
                gain_ctx[me, pl.ds(p, 1)] = jnp.sum(term, axis=0, keepdims=True)
            means = each(lambda term, gain: head_mean(term * gain), terms, gains)
            gatts = [
                ((dy * gain - normed * m) * inv).astype(BF)
                for dy, gain, normed, m, inv in zip(dys, gains, normeds, means, invs)
            ]
            for p, gatt in zip(ps, gatts):
                gatt_s[p] = gatt
            full = each(tn, qbs, gatts)
            for p, x in zip(ps, full):
                back[p] = compact(x)
        backward[0](c).start()
        outcopy(0, c).start()

    chunk_loop(normalize)
    chunk_loop(lambda c: combine(c, backward, back, bnear, bsum, sum_b))

    def gcopy(d, slot):
        return pltpu.make_async_remote_copy(
            src_ref=gain_ctx.at[slot], dst_ref=gain_ctx.at[slot],
            send_sem=gsend.at[d - 1], recv_sem=grecv.at[d - 1],
            device_id={"ctx": lax.rem(me + d, n_ctx)},
        )

    def hcopy(d, slot):
        return pltpu.make_async_remote_copy(
            src_ref=gain_dp.at[slot], dst_ref=gain_dp.at[slot],
            send_sem=hsend.at[d - 1], recv_sem=hrecv.at[d - 1],
            device_id={"dp": lax.rem(mydp + d, n_dp)},
        )

    for d in range(1, n_ctx):
        gcopy(d, me).start()

    def gradients(c):
        for ps in groups(c, 2):
            gatts = [gatt_s[p] for p in ps]
            gss = each(stack, gatts)
            scores = [nt(gs, v_ref[0, :, lanes(p)]) for gs, p in zip(gss, ps)]
            for p, gs in zip(ps, gss):
                gv_s[p] = tn(weights[p], gs)
            gws = [x.astype(BF) * doc_mask[...] for x in scores]
            gqs = [
                nn(jnp.concatenate([gw[:T], gw[T:]], axis=1), stack(k_ref[0, :, lanes(p)]))
                + nt(gatt * masks[2], diag(carried[p]))
                for gw, gatt, p in zip(gws, gatts, ps)
            ]
            for p, gq in zip(ps, gqs):
                gq_ref[0, :, lanes(p)] = gq.astype(BF)
            for p, gw in zip(ps, gws):
                gk_s[p] = tn(gw, stack(q_ref[0, :, lanes(p)]))
        outcopy(1, c).start()

    def gradients_and_relay(c):
        gradients(c)
        for i in range(2):
            relay(2 * c - CHUNKS + i, backward, bbuf, benter, coef_b)

    chunk_loop(gradients, 0, CHUNKS // 2)
    chunk_loop(gradients_and_relay, CHUNKS // 2)

    for d in range(1, n_ctx):
        gcopy(d, lax.rem(me - d + n_ctx, n_ctx)).wait_recv()
    total = gain_ctx[0]
    for i in range(1, n_ctx):
        total += gain_ctx[i]
    gain_dp[mydp] = total
    for d in range(1, n_dp):
        hcopy(d, mydp).start()

    def finish(c):
        backward[3](c).wait_recv()
        for ps in groups(c, 4):
            bds = [diag(gather(bnear, benter, enter_b, p)) for p in ps]
            after = masks[3]
            gks = [nt(v_ref[0, :, lanes(p)] * after, bd) for p, bd in zip(ps, bds)]
            gvs = [nn(k_ref[0, :, lanes(p)] * after, bd) for p, bd in zip(ps, bds)]
            for p, gk, gv in zip(ps, gks, gvs):
                gk_ref[0, :, lanes(p)] = (gk_s[p] + gk).astype(BF)
                gv_ref[0, :, lanes(p)] = (gv_s[p] + gv).astype(BF)
        outcopy(2, c).start()
        outcopy(3, c).start()

    chunk_loop(finish)

    for d in range(1, n_dp):
        hcopy(d, lax.rem(mydp - d + n_dp, n_dp)).wait_recv()
    total = gain_dp[0]
    for i in range(1, n_dp):
        total += gain_dp[i]
    gg_ref[...] = total * (1.0 / math.sqrt(total_tokens))
    gg_copy = pltpu.make_async_copy(gg_ref, gg_hbm, gg_sem)
    gg_copy.start()

    drain(forward)
    drain(backward)
    for d in range(1, n_ctx):
        gcopy(d, me).wait_send()
    for d in range(1, n_dp):
        hcopy(d, mydp).wait_send()
    for i in range(4):
        for c in range(CHUNKS):
            outcopy(i, c).wait()
    gg_copy.wait()


def write_out(*refs):
    sources, targets, held, in_sems, out_sems = refs[:5], refs[5:10], refs[10:15], refs[15], refs[16]

    def copies(from_refs, to_refs, sems):
        made = []
        for i, (source, target) in enumerate(zip(from_refs, to_refs)):
            if i == 4:
                made.append(pltpu.make_async_copy(source, target, sems.at[i, 0]))
                continue
            rows = source.shape[1] // 2
            for h in range(2):
                part = pl.ds(h * rows, rows)
                made.append(
                    pltpu.make_async_copy(source.at[:, part], target.at[:, part], sems.at[i, h])
                )
        return made

    loads, stores = copies(sources, held, in_sems), copies(held, targets, out_sems)
    for load in loads:
        load.start()
    for load, store in zip(loads, stores):
        load.wait()
        store.start()
    for store in stores:
        store.wait()


def per_device(queries, keys, values, grad_output, out_gain, doc_lengths):
    _, T, width = queries.shape
    n_ctx, n_dp = lax.axis_size("ctx"), lax.axis_size("dp")
    length = T * n_ctx
    longest = length // 3
    reach = min(n_ctx // 2 - 1, -(-(longest - 1) // (2 * T)))
    state = pltpu.VMEM((PAIRS, E, LANES), BF)
    far = pltpu.VMEM((reach, PAIRS, E, LANES), BF)
    hbm = pl.BlockSpec(memory_space=pltpu.HBM)
    data = jax.ShapeDtypeStruct((1, T, width), BF)
    dma = pltpu.SemaphoreType.DMA
    hops = [dma((CHUNKS,))] * 2 + [dma((reach, CHUNKS))] * 2 + [dma((CHUNKS,))] * 2
    shapes = (data,) * 4 + (jax.ShapeDtypeStruct((PAIRS, LANES), F32),)
    out = pl.pallas_call(
        functools.partial(kernel, n_ctx, n_dp, reach, n_dp * length),
        out_shape=shapes,
        in_specs=[hbm] * 6,
        out_specs=(hbm,) * 5,
        scratch_shapes=[
            pltpu.SMEM(doc_lengths.shape, jnp.int32),
            pltpu.VMEM((1, T, width), BF),
            pltpu.VMEM((1, T, width), BF),
            pltpu.VMEM((1, T, width), BF),
            pltpu.VMEM((1, T, width), BF),
            pltpu.VMEM((1, width), F32),
            dma((4, CHUNKS)),
            dma((2,)),
            pltpu.VMEM((1, T, width), BF),
            pltpu.VMEM((1, T, width), BF),
            pltpu.VMEM((1, T, width), BF),
            pltpu.VMEM((1, T, width), BF),
            pltpu.VMEM((PAIRS, LANES), F32),
            dma((4, CHUNKS)),
            dma,
            pltpu.VMEM((4, T, LANES), BF),
            pltpu.VMEM((2 * T, T), BF),
            state, state, state, state, state, state,
            far, far, state, state, state,
            pltpu.VMEM((PAIRS, 2 * T, T), BF),
            pltpu.VMEM((PAIRS, T, LANES), F32),
            pltpu.VMEM((PAIRS, T, LANES), BF),
            pltpu.VMEM((PAIRS, T, LANES), F32),
            pltpu.VMEM((PAIRS, T, LANES), F32),
            pltpu.VMEM((n_ctx, PAIRS, LANES), F32),
            pltpu.VMEM((n_dp, PAIRS, LANES), F32),
            hops, hops,
            dma((n_ctx - 1,)), dma((n_ctx - 1,)),
            dma((n_dp - 1,)), dma((n_dp - 1,)),
        ],
        compiler_params=pltpu.CompilerParams(
            collective_id=0, has_side_effects=True, vmem_limit_bytes=VMEM_LIMIT
        ),
    )(doc_lengths, queries, keys, values, grad_output, out_gain.reshape(1, width))
    out = pl.pallas_call(
        write_out,
        out_shape=shapes,
        in_specs=[hbm] * 5,
        out_specs=(hbm,) * 5,
        scratch_shapes=[pltpu.VMEM(x.shape, x.dtype) for x in shapes]
        + [dma((5, 2)), dma((5, 2))],
        compiler_params=pltpu.CompilerParams(vmem_limit_bytes=VMEM_LIMIT),
    )(*out)
    return (*out[:4], out[4].reshape(width))


def solution(mesh):
    seq = P("dp", "ctx", None)
    return jax.shard_map(
        per_device,
        mesh=mesh,
        in_specs=(seq, seq, seq, seq, P(), P("dp", None)),
        out_specs=(seq, seq, seq, seq, P()),
        check_vma=False,
    )
```

```python
import functools
import math

import jax
import jax.numpy as jnp
from jax import lax
from jax.experimental import pallas as pl
from jax.experimental.pallas import tpu as pltpu
from jax.sharding import PartitionSpec as P

H = 32
E = 64
LANES = 2 * E
PAIRS = H // 2
CHUNKS = 4
PER = PAIRS // CHUNKS
HALF = PER // 2
EPS = 1e-05
VMEM_LIMIT = 58 * 1024 * 1024
BF = jnp.bfloat16
F32 = jnp.float32


def nn(a, b):
    return lax.dot_general(a, b, (((1,), (0,)), ((), ())), preferred_element_type=F32)


def nt(a, b):
    return lax.dot_general(a, b, (((1,), (1,)), ((), ())), preferred_element_type=F32)


def tn(a, b):
    return lax.dot_general(a, b, (((0,), (0,)), ((), ())), preferred_element_type=F32)


def kernel(
    n_ctx, n_dp, reach, total_tokens,
    lengths_hbm, q_hbm, k_hbm, v_hbm, dy_hbm, gain_hbm,
    out_hbm, gq_hbm, gk_hbm, gv_hbm, gg_hbm,
    lengths_ref, q_ref, k_ref, v_ref, dy_ref, gain_ref, in_sem, small_sem,
    out_ref, gq_ref, gk_ref, gv_ref, gg_ref, out_sem, gg_sem,
    masks, doc_mask, own, back, fnear, bnear, fsum, bsum, fbuf, bbuf, fenter, benter, carried, weights, att_s, gatt_s, gk_s, gv_s,
    gain_ctx, gain_dp,
    fsems, bsems, gsend, grecv, hsend, hrecv,
):
    me = lax.axis_index("ctx")
    chip, side = me // 2, lax.rem(me, 2)
    partner = me + 1 - 2 * side
    n_chips = n_ctx // 2
    mydp = lax.axis_index("dp")
    T = q_ref.shape[1]

    small = [
        pltpu.make_async_copy(lengths_hbm, lengths_ref, small_sem.at[0]),
        pltpu.make_async_copy(gain_hbm, gain_ref, small_sem.at[1]),
    ]

    def incopy(i, c):
        source, target = ((k_hbm, k_ref), (v_hbm, v_ref), (q_hbm, q_ref), (dy_hbm, dy_ref))[i]
        part = pl.ds(pl.multiple_of(c * (PER * LANES), PER * LANES), PER * LANES)
        return pltpu.make_async_copy(
            source.at[:, :, part], target.at[:, :, part], in_sem.at[i, c]
        )

    def outcopy(i, c):
        source, target = (
            (out_ref, out_hbm), (gq_ref, gq_hbm), (gk_ref, gk_hbm), (gv_ref, gv_hbm)
        )[i]
        part = pl.ds(pl.multiple_of(c * (PER * LANES), PER * LANES), PER * LANES)
        return pltpu.make_async_copy(
            source.at[:, :, part], target.at[:, :, part], out_sem.at[i, c]
        )

    small[0].start()
    for c in range(CHUNKS):
        incopy(0, c).start()
        incopy(1, c).start()
    for c in range(CHUNKS):
        incopy(2, c).start()
    small[1].start()
    for c in range(CHUNKS):
        incopy(3, c).start()

    barrier = pltpu.get_barrier_semaphore()
    for d in range(1, n_ctx):
        pl.semaphore_signal(barrier, inc=1, device_id={"ctx": lax.rem(me + d, n_ctx)})
    for d in range(1, n_dp):
        pl.semaphore_signal(barrier, inc=1, device_id={"dp": lax.rem(mydp + d, n_dp)})

    small[0].wait()
    docs = lengths_ref.shape[1]
    offset = me * T
    first, last = jnp.int32(1 << 20), jnp.int32(-(1 << 20))
    hits_even, hits_odd = jnp.int32(0), jnp.int32(0)
    hits_f = [jnp.int32(0)] * (reach + 1)
    hits_b = [jnp.int32(0)] * (reach + 1)
    row = lax.broadcasted_iota(jnp.int32, (T, T), 0)
    col = lax.broadcasted_iota(jnp.int32, (T, T), 1)
    id_row = jnp.zeros((T, T), jnp.int32)
    id_col = jnp.zeros((T, T), jnp.int32)
    begin = -offset
    for i in range(docs):
        first = jnp.where(begin >= 0, jnp.minimum(first, begin), first)
        last = jnp.where(begin < T, jnp.maximum(last, begin), last)
        base = begin + side * T
        for d in range(2, reach + 1):
            hits_f[d] += jnp.where((base >= -(d - 1) * 2 * T) & (base < 0), 1, 0)
            hits_b[d] += jnp.where((base >= 2 * T) & (base < d * 2 * T), 1, 0)
        hits_even += jnp.where((base >= 0) & (base < T), 1, 0)
        hits_odd += jnp.where((base >= T) & (base < 2 * T), 1, 0)
        id_row += (row >= begin).astype(jnp.int32)
        id_col += (col >= begin).astype(jnp.int32)
        begin = begin + lengths_ref[0, i]
    coef_f = [jnp.where(hits_f[d] == 0, 1.0, 0.0).astype(F32) for d in range(reach + 1)]
    coef_b = [jnp.where(hits_b[d] == 0, 1.0, 0.0).astype(F32) for d in range(reach + 1)]
    keep_even = jnp.where(hits_even == 0, 1.0, 0.0).astype(F32)
    keep_odd = jnp.where(hits_odd == 0, 1.0, 0.0).astype(F32)
    odd = jnp.where(side == 1, 1.0, 0.0).astype(F32)
    sum_f = (odd + (1.0 - odd) * keep_odd, (1.0 - odd) + odd * keep_odd)
    sum_b = ((1.0 - odd) + odd * keep_even, odd + (1.0 - odd) * keep_even)
    enter_f = (odd, (1.0 - odd) + odd * keep_even)
    enter_b = (1.0 - odd, odd + (1.0 - odd) * keep_odd)
    dm = jnp.where((row >= col) & (id_row == id_col), 1.0, 0.0).astype(BF)
    doc_mask[0:T] = dm
    doc_mask[T:2 * T] = dm
    trow = lax.broadcasted_iota(jnp.int32, (T, LANES), 0)
    lane = lax.broadcasted_iota(jnp.int32, (T, LANES), 1)
    masks[0] = jnp.where(lane < E, 1.0, 0.0).astype(BF)
    masks[1] = jnp.where(lane < E, 0.0, 1.0).astype(BF)
    masks[2] = jnp.where(trow < first, 1.0, 0.0).astype(BF)
    masks[3] = jnp.where(trow >= last, 1.0, 0.0).astype(BF)

    for d in range(1, reach + 1):
        @pl.when(chip - d < 0)
        def _():
            fbuf[d - 1] = jnp.zeros(fbuf.shape[1:], BF)

        @pl.when(chip + d >= n_chips)
        def _():
            bbuf[d - 1] = jnp.zeros(bbuf.shape[1:], BF)

    def lanes(p):
        return pl.ds(pl.multiple_of(p * LANES, LANES), LANES)

    def compact(full):
        left = lax.broadcasted_iota(jnp.int32, (E, LANES), 1) < E
        return jnp.where(left, full[:E], full[E:]).astype(BF)

    def diag(c):
        return jnp.concatenate([c * masks[0, 0:E], c * masks[1, 0:E]], axis=0)

    def stack(x):
        return jnp.concatenate([x * masks[0], x * masks[1]], axis=0)

    def whole(c):
        return pl.ds(c * PER, PER)

    def mine(c):
        return pl.ds(c * PER + side * HALF, HALF)

    def links(state, near, summed, buf, enter, sems, sign):
        send, recv, far_send, far_recv, last_send, last_recv = sems

        def first_hop(c):
            return pltpu.make_async_remote_copy(
                src_ref=state.at[whole(c)], dst_ref=near.at[whole(c)],
                send_sem=send.at[c], recv_sem=recv.at[c], device_id={"ctx": partner},
            )

        def far_hop(d, c):
            return pltpu.make_async_remote_copy(
                src_ref=summed.at[mine(c)], dst_ref=buf.at[d - 1, mine(c)],
                send_sem=far_send.at[d - 1, c], recv_sem=far_recv.at[d - 1, c],
                device_id={"ctx": lax.rem(me + sign * 2 * d + n_ctx, n_ctx)},
            )

        def last_hop(c):
            return pltpu.make_async_remote_copy(
                src_ref=enter.at[mine(c)], dst_ref=enter.at[mine(c)],
                send_sem=last_send.at[c], recv_sem=last_recv.at[c],
                device_id={"ctx": partner},
            )

        def other_last_hop(c):
            theirs = pl.ds(c * PER + (1 - side) * HALF, HALF)
            return pltpu.make_async_remote_copy(
                src_ref=enter.at[theirs], dst_ref=enter.at[theirs],
                send_sem=last_send.at[c], recv_sem=last_recv.at[c],
                device_id={"ctx": partner},
            )

        def sends(d):
            return chip + d < n_chips if sign > 0 else chip - d >= 0

        def gets(d):
            return chip - d >= 0 if sign > 0 else chip + d < n_chips

        return first_hop, far_hop, last_hop, other_last_hop, sends, gets

    forward = links(own, fnear, fsum, fbuf, fenter, fsems, 1)
    backward = links(back, bnear, bsum, bbuf, benter, bsems, -1)

    def combine(c, link, state, near, summed, take):
        first_hop, far_hop, _, _, sends, _ = link
        first_hop(c).wait_recv()
        x = state[mine(c)].astype(F32) * take[0] + near[mine(c)].astype(F32) * take[1]
        summed[mine(c)] = x.astype(BF)
        for d in range(1, reach + 1):
            @pl.when(sends(d))
            def _():
                far_hop(d, c).start()

    def relay(c, link, buf, enter, coef):
        _, far_hop, last_hop, _, _, gets = link
        for d in range(1, reach + 1):
            @pl.when(gets(d))
            def _():
                far_hop(d, c).wait_recv()
        x = buf[0, mine(c)].astype(F32) * coef[1]
        for d in range(2, reach + 1):
            x += buf[d - 1, mine(c)].astype(F32) * coef[d]
        enter[mine(c)] = x.astype(BF)
        last_hop(c).start()

    def combine_forward(c):
        combine(c, forward, own, fnear, fsum, sum_f)

    def combine_backward(c):
        combine(c, backward, back, bnear, bsum, sum_b)

    def relay_forward(c):
        relay(c, forward, fbuf, fenter, coef_f)

    def relay_backward(c):
        relay(c, backward, bbuf, benter, coef_b)

    def exchange(c, combine_one, relay_one):
        @pl.when(c == 0)
        def _():
            combine_one(CHUNKS - 1)

        @pl.when(c > 0)
        def _():
            relay_one(c - 1)

    def drain(link):
        first_hop, far_hop, last_hop, _, sends, _ = link
        for c in range(CHUNKS):
            first_hop(c).wait_send()
            last_hop(c).wait_send()
            for d in range(1, reach + 1):
                @pl.when(sends(d))
                def _():
                    far_hop(d, c).wait_send()

    def each(f, *lists):
        return [f(*items) for items in zip(*lists)]

    def chunk_loop(body, low=0, high=CHUNKS):
        def step(c, _):
            body(c)
            return 0
        lax.fori_loop(low, high, step, 0)

    def groups(c, size):
        return [[c * PER + g + i for i in range(size)] for g in range(0, PER, size)]

    def states(c):
        incopy(0, c).wait()
        incopy(1, c).wait()
        for ps in groups(c, 4):
            ks = [k_ref[0, :, lanes(p)] * masks[3] for p in ps]
            full = [tn(k, v_ref[0, :, lanes(p)]) for k, p in zip(ks, ps)]
            for p, x in zip(ps, full):
                own[p] = compact(x)

        @pl.when(c == 0)
        def _():
            pl.semaphore_wait(barrier, n_ctx + n_dp - 2)

        forward[0](c).start()

        @pl.when(c > 0)
        def _():
            combine_forward(c - 1)

    chunk_loop(states)

    def inside(c):
        incopy(2, c).wait()
        for ps in groups(c, 2):
            qs = [stack(q_ref[0, :, lanes(p)]) for p in ps]
            scores = [nt(q, k_ref[0, :, lanes(p)]) for q, p in zip(qs, ps)]
            ws = [x.astype(BF) * doc_mask[...] for x in scores]
            for p, w in zip(ps, ws):
                weights[p] = w
            atts = [
                nn(jnp.concatenate([w[:T], w[T:]], axis=1), stack(v_ref[0, :, lanes(p)]))
                for w, p in zip(ws, ps)
            ]
            for p, att in zip(ps, atts):
                att_s[p] = att
        exchange(c, combine_forward, relay_forward)

    chunk_loop(inside)
    relay_forward(CHUNKS - 1)

    jrow = lax.broadcasted_iota(jnp.int32, (2 * LANES, LANES), 0)
    jlane = lax.broadcasted_iota(jnp.int32, (2 * LANES, LANES), 1)
    mean_of = jnp.where((lax.rem(jrow, LANES) < E) == (jlane < E), 1.0 / E, 0.0).astype(BF)

    def head_means(xs):
        x = jnp.concatenate(xs, axis=0)
        high = x.astype(BF)
        low = (x - high.astype(F32)).astype(BF)
        means = nn(jnp.concatenate([high, low], axis=1), mean_of)
        return [means[i * T:(i + 1) * T] for i in range(len(xs))]

    def gather(near, enter, take, p):
        return (near[p].astype(F32) * take[0] + enter[p].astype(F32) * take[1]).astype(BF)

    small[1].wait()

    def normalize(c):
        forward[3](c).wait_recv()
        incopy(3, c).wait()
        for ps in groups(c, 4):
            cs = [gather(fnear, fenter, enter_f, p) for p in ps]
            for p, x in zip(ps, cs):
                carried[p] = x
            qbs = [q_ref[0, :, lanes(p)] * masks[2] for p in ps]
            atts = [att_s[p] + nn(qb, diag(x)) for p, qb, x in zip(ps, qbs, cs)]
            means = head_means([att * att for att in atts])
            invs = [lax.rsqrt(m + EPS) for m in means]
            normeds = each(lambda att, inv: att * inv, atts, invs)
            gains = [gain_ref[:, lanes(p)] for p in ps]
            for p, gain, normed in zip(ps, gains, normeds):
                out_ref[0, :, lanes(p)] = (gain * normed).astype(BF)
            dys = [dy_ref[0, :, lanes(p)].astype(F32) for p in ps]
            terms = each(lambda dy, normed: dy * normed, dys, normeds)
            for p, term in zip(ps, terms):
                gain_ctx[me, pl.ds(p, 1)] = jnp.sum(term, axis=0, keepdims=True)
            means = head_means(each(lambda term, gain: term * gain, terms, gains))
            gatts = [
                ((dy * gain - normed * m) * inv).astype(BF)
                for dy, gain, normed, m, inv in zip(dys, gains, normeds, means, invs)
            ]
            for p, gatt in zip(ps, gatts):
                gatt_s[p] = gatt
            full = each(tn, qbs, gatts)
            for p, x in zip(ps, full):
                back[p] = compact(x)
        backward[0](c).start()
        outcopy(0, c).start()

        @pl.when(c > 0)
        def _():
            combine_backward(c - 1)

    chunk_loop(normalize)

    def gcopy(d, slot):
        return pltpu.make_async_remote_copy(
            src_ref=gain_ctx.at[slot], dst_ref=gain_ctx.at[slot],
            send_sem=gsend.at[d - 1], recv_sem=grecv.at[d - 1],
            device_id={"ctx": lax.rem(me + d, n_ctx)},
        )

    def hcopy(d, slot):
        return pltpu.make_async_remote_copy(
            src_ref=gain_dp.at[slot], dst_ref=gain_dp.at[slot],
            send_sem=hsend.at[d - 1], recv_sem=hrecv.at[d - 1],
            device_id={"dp": lax.rem(mydp + d, n_dp)},
        )

    for d in range(1, n_ctx):
        gcopy(d, me).start()

    def gradients(c):
        for ps in groups(c, 2):
            gatts = [gatt_s[p] for p in ps]
            gss = each(stack, gatts)
            scores = [nt(gs, v_ref[0, :, lanes(p)]) for gs, p in zip(gss, ps)]
            for p, gs in zip(ps, gss):
                gv_s[p] = tn(weights[p], gs)
            gws = [x.astype(BF) * doc_mask[...] for x in scores]
            gqs = [
                nn(jnp.concatenate([gw[:T], gw[T:]], axis=1), stack(k_ref[0, :, lanes(p)]))
                + nt(gatt * masks[2], diag(carried[p]))
                for gw, gatt, p in zip(gws, gatts, ps)
            ]
            for p, gq in zip(ps, gqs):
                gq_ref[0, :, lanes(p)] = gq.astype(BF)
            for p, gw in zip(ps, gws):
                gk_s[p] = tn(gw, stack(q_ref[0, :, lanes(p)]))
        outcopy(1, c).start()
        exchange(c, combine_backward, relay_backward)

    chunk_loop(gradients)
    relay_backward(CHUNKS - 1)

    for d in range(1, n_ctx):
        gcopy(d, lax.rem(me - d + n_ctx, n_ctx)).wait_recv()
    total = gain_ctx[0]
    for i in range(1, n_ctx):
        total += gain_ctx[i]
    gain_dp[mydp] = total
    for d in range(1, n_dp):
        hcopy(d, mydp).start()

    def finish(c):
        backward[3](c).wait_recv()
        for ps in groups(c, 4):
            bds = [diag(gather(bnear, benter, enter_b, p)) for p in ps]
            after = masks[3]
            gks = [nt(v_ref[0, :, lanes(p)] * after, bd) for p, bd in zip(ps, bds)]
            gvs = [nn(k_ref[0, :, lanes(p)] * after, bd) for p, bd in zip(ps, bds)]
            for p, gk, gv in zip(ps, gks, gvs):
                gk_ref[0, :, lanes(p)] = (gk_s[p] + gk).astype(BF)
                gv_ref[0, :, lanes(p)] = (gv_s[p] + gv).astype(BF)
        outcopy(2, c).start()
        outcopy(3, c).start()

    chunk_loop(finish)

    for d in range(1, n_dp):
        hcopy(d, lax.rem(mydp - d + n_dp, n_dp)).wait_recv()
    total = gain_dp[0]
    for i in range(1, n_dp):
        total += gain_dp[i]
    gg_ref[...] = total * (1.0 / math.sqrt(total_tokens))
    gg_copy = pltpu.make_async_copy(gg_ref, gg_hbm, gg_sem)
    gg_copy.start()

    drain(forward)
    drain(backward)
    for d in range(1, n_ctx):
        gcopy(d, me).wait_send()
    for d in range(1, n_dp):
        hcopy(d, mydp).wait_send()
    for i in range(4):
        for c in range(CHUNKS):
            outcopy(i, c).wait()
    gg_copy.wait()


def write_out(*refs):
    sources, targets, held, in_sems, out_sems = refs[:5], refs[5:10], refs[10:15], refs[15], refs[16]

    def copies(from_refs, to_refs, sems):
        made = []
        for i, (source, target) in enumerate(zip(from_refs, to_refs)):
            if i == 4:
                made.append(pltpu.make_async_copy(source, target, sems.at[i, 0]))
                continue
            rows = source.shape[1] // 2
            for h in range(2):
                part = pl.ds(h * rows, rows)
                made.append(
                    pltpu.make_async_copy(source.at[:, part], target.at[:, part], sems.at[i, h])
                )
        return made

    loads, stores = copies(sources, held, in_sems), copies(held, targets, out_sems)
    for load in loads:
        load.start()
    for load, store in zip(loads, stores):
        load.wait()
        store.start()
    for store in stores:
        store.wait()


def per_device(queries, keys, values, grad_output, out_gain, doc_lengths):
    _, T, width = queries.shape
    n_ctx, n_dp = lax.axis_size("ctx"), lax.axis_size("dp")
    length = T * n_ctx
    longest = length // 3
    reach = min(n_ctx // 2 - 1, -(-(longest - 1) // (2 * T)))
    state = pltpu.VMEM((PAIRS, E, LANES), BF)
    far = pltpu.VMEM((reach, PAIRS, E, LANES), BF)
    hbm = pl.BlockSpec(memory_space=pltpu.HBM)
    data = jax.ShapeDtypeStruct((1, T, width), BF)
    dma = pltpu.SemaphoreType.DMA
    hops = [dma((CHUNKS,))] * 2 + [dma((reach, CHUNKS))] * 2 + [dma((CHUNKS,))] * 2
    shapes = (data,) * 4 + (jax.ShapeDtypeStruct((PAIRS, LANES), F32),)
    out = pl.pallas_call(
        functools.partial(kernel, n_ctx, n_dp, reach, n_dp * length),
        out_shape=shapes,
        in_specs=[hbm] * 6,
        out_specs=(hbm,) * 5,
        scratch_shapes=[
            pltpu.SMEM(doc_lengths.shape, jnp.int32),
            pltpu.VMEM((1, T, width), BF),
            pltpu.VMEM((1, T, width), BF),
            pltpu.VMEM((1, T, width), BF),
            pltpu.VMEM((1, T, width), BF),
            pltpu.VMEM((1, width), F32),
            dma((4, CHUNKS)),
            dma((2,)),
            pltpu.VMEM((1, T, width), BF),
            pltpu.VMEM((1, T, width), BF),
            pltpu.VMEM((1, T, width), BF),
            pltpu.VMEM((1, T, width), BF),
            pltpu.VMEM((PAIRS, LANES), F32),
            dma((4, CHUNKS)),
            dma,
            pltpu.VMEM((4, T, LANES), BF),
            pltpu.VMEM((2 * T, T), BF),
            state, state, state, state, state, state,
            far, far, state, state, state,
            pltpu.VMEM((PAIRS, 2 * T, T), BF),
            pltpu.VMEM((PAIRS, T, LANES), F32),
            pltpu.VMEM((PAIRS, T, LANES), BF),
            pltpu.VMEM((PAIRS, T, LANES), F32),
            pltpu.VMEM((PAIRS, T, LANES), F32),
            pltpu.VMEM((n_ctx, PAIRS, LANES), F32),
            pltpu.VMEM((n_dp, PAIRS, LANES), F32),
            hops, hops,
            dma((n_ctx - 1,)), dma((n_ctx - 1,)),
            dma((n_dp - 1,)), dma((n_dp - 1,)),
        ],
        compiler_params=pltpu.CompilerParams(
            collective_id=0, has_side_effects=True, vmem_limit_bytes=VMEM_LIMIT
        ),
    )(doc_lengths, queries, keys, values, grad_output, out_gain.reshape(1, width))
    out = pl.pallas_call(
        write_out,
        out_shape=shapes,
        in_specs=[hbm] * 5,
        out_specs=(hbm,) * 5,
        scratch_shapes=[pltpu.VMEM(x.shape, x.dtype) for x in shapes]
        + [dma((5, 2)), dma((5, 2))],
        compiler_params=pltpu.CompilerParams(vmem_limit_bytes=VMEM_LIMIT),
    )(*out)
    return (*out[:4], out[4].reshape(width))


def solution(mesh):
    seq = P("dp", "ctx", None)
    return jax.shard_map(
        per_device,
        mesh=mesh,
        in_specs=(seq, seq, seq, seq, P(), P("dp", None)),
        out_specs=(seq, seq, seq, seq, P()),
        check_vma=False,
    )
```

```python
import functools
import math

import jax
import jax.numpy as jnp
from jax import lax
from jax.experimental import pallas as pl
from jax.experimental.pallas import tpu as pltpu
from jax.sharding import PartitionSpec as P

H = 32
E = 64
LANES = 2 * E
PAIRS = H // 2
CHUNKS = 4
PER = PAIRS // CHUNKS
HALF = PER // 2
EPS = 1e-05
VMEM_LIMIT = 58 * 1024 * 1024
BF = jnp.bfloat16
F32 = jnp.float32


def nn(a, b):
    return lax.dot_general(a, b, (((1,), (0,)), ((), ())), preferred_element_type=F32)


def nt(a, b):
    return lax.dot_general(a, b, (((1,), (1,)), ((), ())), preferred_element_type=F32)


def tn(a, b):
    return lax.dot_general(a, b, (((0,), (0,)), ((), ())), preferred_element_type=F32)


def kernel(
    n_ctx, n_dp, reach, total_tokens,
    lengths_hbm, q_hbm, k_hbm, v_hbm, dy_hbm, gain_hbm,
    out_hbm, gq_hbm, gk_hbm, gv_hbm, gg_hbm,
    lengths_ref, q_ref, k_ref, v_ref, dy_ref, gain_ref, in_sem, small_sem,
    out_ref, gq_ref, gk_ref, gv_ref, gg_ref, out_sem, gg_sem,
    masks, doc_mask, own, back, fnear, bnear, fsum, bsum, fbuf, bbuf, fenter, benter, carried, weights, att_s, gatt_s, gk_s, gv_s,
    gain_ctx, gain_dp,
    fsems, bsems, gsend, grecv, hsend, hrecv,
):
    me = lax.axis_index("ctx")
    chip, side = me // 2, lax.rem(me, 2)
    partner = me + 1 - 2 * side
    n_chips = n_ctx // 2
    mydp = lax.axis_index("dp")
    T = q_ref.shape[1]

    small = [
        pltpu.make_async_copy(lengths_hbm, lengths_ref, small_sem.at[0]),
        pltpu.make_async_copy(gain_hbm, gain_ref, small_sem.at[1]),
    ]

    def incopy(i, c):
        source, target = ((k_hbm, k_ref), (v_hbm, v_ref), (q_hbm, q_ref), (dy_hbm, dy_ref))[i]
        part = pl.ds(pl.multiple_of(c * (PER * LANES), PER * LANES), PER * LANES)
        return pltpu.make_async_copy(
            source.at[:, :, part], target.at[:, :, part], in_sem.at[i, c]
        )

    def outcopy(i, c):
        source, target = (
            (out_ref, out_hbm), (gq_ref, gq_hbm), (gk_ref, gk_hbm), (gv_ref, gv_hbm)
        )[i]
        part = pl.ds(pl.multiple_of(c * (PER * LANES), PER * LANES), PER * LANES)
        return pltpu.make_async_copy(
            source.at[:, :, part], target.at[:, :, part], out_sem.at[i, c]
        )

    small[0].start()
    for c in range(CHUNKS):
        incopy(0, c).start()
        incopy(1, c).start()
    for c in range(CHUNKS):
        incopy(2, c).start()
    small[1].start()
    for c in range(CHUNKS):
        incopy(3, c).start()

    barrier = pltpu.get_barrier_semaphore()
    for d in range(1, n_ctx):
        pl.semaphore_signal(barrier, inc=1, device_id={"ctx": lax.rem(me + d, n_ctx)})
    for d in range(1, n_dp):
        pl.semaphore_signal(barrier, inc=1, device_id={"dp": lax.rem(mydp + d, n_dp)})

    small[0].wait()
    docs = lengths_ref.shape[1]
    offset = me * T
    first, last = jnp.int32(1 << 20), jnp.int32(-(1 << 20))
    hits_even, hits_odd = jnp.int32(0), jnp.int32(0)
    hits_f = [jnp.int32(0)] * (reach + 1)
    hits_b = [jnp.int32(0)] * (reach + 1)
    row = lax.broadcasted_iota(jnp.int32, (T, T), 0)
    col = lax.broadcasted_iota(jnp.int32, (T, T), 1)
    id_row = jnp.zeros((T, T), jnp.int32)
    id_col = jnp.zeros((T, T), jnp.int32)
    begin = -offset
    for i in range(docs):
        first = jnp.where(begin >= 0, jnp.minimum(first, begin), first)
        last = jnp.where(begin < T, jnp.maximum(last, begin), last)
        base = begin + side * T
        for d in range(2, reach + 1):
            hits_f[d] += jnp.where((base >= -(d - 1) * 2 * T) & (base < 0), 1, 0)
            hits_b[d] += jnp.where((base >= 2 * T) & (base < d * 2 * T), 1, 0)
        hits_even += jnp.where((base >= 0) & (base < T), 1, 0)
        hits_odd += jnp.where((base >= T) & (base < 2 * T), 1, 0)
        id_row += (row >= begin).astype(jnp.int32)
        id_col += (col >= begin).astype(jnp.int32)
        begin = begin + lengths_ref[0, i]
    coef_f = [jnp.where(hits_f[d] == 0, 1.0, 0.0).astype(F32) for d in range(reach + 1)]
    coef_b = [jnp.where(hits_b[d] == 0, 1.0, 0.0).astype(F32) for d in range(reach + 1)]
    keep_even = jnp.where(hits_even == 0, 1.0, 0.0).astype(F32)
    keep_odd = jnp.where(hits_odd == 0, 1.0, 0.0).astype(F32)
    odd = jnp.where(side == 1, 1.0, 0.0).astype(F32)
    sum_f = (odd + (1.0 - odd) * keep_odd, (1.0 - odd) + odd * keep_odd)
    sum_b = ((1.0 - odd) + odd * keep_even, odd + (1.0 - odd) * keep_even)
    enter_f = (odd, (1.0 - odd) + odd * keep_even)
    enter_b = (1.0 - odd, odd + (1.0 - odd) * keep_odd)
    dm = jnp.where((row >= col) & (id_row == id_col), 1.0, 0.0).astype(BF)
    doc_mask[0:T] = dm
    doc_mask[T:2 * T] = dm
    trow = lax.broadcasted_iota(jnp.int32, (T, LANES), 0)
    lane = lax.broadcasted_iota(jnp.int32, (T, LANES), 1)
    masks[0] = jnp.where(lane < E, 1.0, 0.0).astype(BF)
    masks[1] = jnp.where(lane < E, 0.0, 1.0).astype(BF)
    masks[2] = jnp.where(trow < first, 1.0, 0.0).astype(BF)
    masks[3] = jnp.where(trow >= last, 1.0, 0.0).astype(BF)

    for d in range(1, reach + 1):
        @pl.when(chip - d < 0)
        def _():
            fbuf[d - 1] = jnp.zeros(fbuf.shape[1:], BF)

        @pl.when(chip + d >= n_chips)
        def _():
            bbuf[d - 1] = jnp.zeros(bbuf.shape[1:], BF)

    def lanes(p):
        return pl.ds(pl.multiple_of(p * LANES, LANES), LANES)

    def compact(full):
        left = lax.broadcasted_iota(jnp.int32, (E, LANES), 1) < E
        return jnp.where(left, full[:E], full[E:]).astype(BF)

    def diag(c):
        return jnp.concatenate([c * masks[0, 0:E], c * masks[1, 0:E]], axis=0)

    def stack(x):
        return jnp.concatenate([x * masks[0], x * masks[1]], axis=0)

    def whole(c):
        return pl.ds(c * PER, PER)

    def mine(c):
        return pl.ds(c * PER + side * HALF, HALF)

    def links(state, near, summed, buf, enter, sems, sign):
        send, recv, far_send, far_recv, last_send, last_recv = sems

        def first_hop(c):
            return pltpu.make_async_remote_copy(
                src_ref=state.at[whole(c)], dst_ref=near.at[whole(c)],
                send_sem=send.at[c], recv_sem=recv.at[c], device_id={"ctx": partner},
            )

        def far_hop(d, c):
            return pltpu.make_async_remote_copy(
                src_ref=summed.at[mine(c)], dst_ref=buf.at[d - 1, mine(c)],
                send_sem=far_send.at[d - 1, c], recv_sem=far_recv.at[d - 1, c],
                device_id={"ctx": lax.rem(me + sign * 2 * d + n_ctx, n_ctx)},
            )

        def last_hop(c):
            return pltpu.make_async_remote_copy(
                src_ref=enter.at[mine(c)], dst_ref=enter.at[mine(c)],
                send_sem=last_send.at[c], recv_sem=last_recv.at[c],
                device_id={"ctx": partner},
            )

        def other_last_hop(c):
            theirs = pl.ds(c * PER + (1 - side) * HALF, HALF)
            return pltpu.make_async_remote_copy(
                src_ref=enter.at[theirs], dst_ref=enter.at[theirs],
                send_sem=last_send.at[c], recv_sem=last_recv.at[c],
                device_id={"ctx": partner},
            )

        def sends(d):
            return chip + d < n_chips if sign > 0 else chip - d >= 0

        def gets(d):
            return chip - d >= 0 if sign > 0 else chip + d < n_chips

        return first_hop, far_hop, last_hop, other_last_hop, sends, gets

    forward = links(own, fnear, fsum, fbuf, fenter, fsems, 1)
    backward = links(back, bnear, bsum, bbuf, benter, bsems, -1)

    def combine(c, link, state, near, summed, take):
        first_hop, far_hop, _, _, sends, _ = link
        first_hop(c).wait_recv()
        x = state[mine(c)].astype(F32) * take[0] + near[mine(c)].astype(F32) * take[1]
        summed[mine(c)] = x.astype(BF)
        for d in range(1, reach + 1):
            @pl.when(sends(d))
            def _():
                far_hop(d, c).start()

    def relay(c, link, buf, enter, coef):
        _, far_hop, last_hop, _, _, gets = link
        for d in range(1, reach + 1):
            @pl.when(gets(d))
            def _():
                far_hop(d, c).wait_recv()
        x = buf[0, mine(c)].astype(F32) * coef[1]
        for d in range(2, reach + 1):
            x += buf[d - 1, mine(c)].astype(F32) * coef[d]
        enter[mine(c)] = x.astype(BF)
        last_hop(c).start()

    def combine_forward(c):
        combine(c, forward, own, fnear, fsum, sum_f)

    def combine_backward(c):
        combine(c, backward, back, bnear, bsum, sum_b)

    def relay_forward(c):
        relay(c, forward, fbuf, fenter, coef_f)

    def relay_backward(c):
        relay(c, backward, bbuf, benter, coef_b)

    def exchange(c, combine_one, relay_one):
        @pl.when(c == 0)
        def _():
            combine_one(CHUNKS - 1)

        @pl.when(c > 0)
        def _():
            relay_one(c - 1)

    def drain(link):
        first_hop, far_hop, last_hop, _, sends, _ = link
        for c in range(CHUNKS):
            first_hop(c).wait_send()
            last_hop(c).wait_send()
            for d in range(1, reach + 1):
                @pl.when(sends(d))
                def _():
                    far_hop(d, c).wait_send()

    def each(f, *lists):
        return [f(*items) for items in zip(*lists)]

    def chunk_loop(body, low=0, high=CHUNKS):
        def step(c, _):
            body(c)
            return 0
        lax.fori_loop(low, high, step, 0)

    def groups(c, size):
        return [[c * PER + g + i for i in range(size)] for g in range(0, PER, size)]

    def states(c):
        incopy(0, c).wait()
        incopy(1, c).wait()
        for ps in groups(c, 4):
            ks = [k_ref[0, :, lanes(p)] * masks[3] for p in ps]
            full = [tn(k, v_ref[0, :, lanes(p)]) for k, p in zip(ks, ps)]
            for p, x in zip(ps, full):
                own[p] = compact(x)

        @pl.when(c == 0)
        def _():
            pl.semaphore_wait(barrier, n_ctx + n_dp - 2)

        forward[0](c).start()

        @pl.when(c > 0)
        def _():
            combine_forward(c - 1)

    chunk_loop(states)

    def inside(c):
        incopy(2, c).wait()
        for ps in groups(c, 4):
            qs = [stack(q_ref[0, :, lanes(p)]) for p in ps]
            scores = [nt(q, k_ref[0, :, lanes(p)]) for q, p in zip(qs, ps)]
            ws = [x.astype(BF) * doc_mask[...] for x in scores]
            for p, w in zip(ps, ws):
                weights[p] = w
            atts = [
                nn(jnp.concatenate([w[:T], w[T:]], axis=1), stack(v_ref[0, :, lanes(p)]))
                for w, p in zip(ws, ps)
            ]
            for p, att in zip(ps, atts):
                att_s[p] = att
        exchange(c, combine_forward, relay_forward)

    chunk_loop(inside)
    relay_forward(CHUNKS - 1)

    jrow = lax.broadcasted_iota(jnp.int32, (2 * LANES, LANES), 0)
    jlane = lax.broadcasted_iota(jnp.int32, (2 * LANES, LANES), 1)
    mean_of = jnp.where((lax.rem(jrow, LANES) < E) == (jlane < E), 1.0 / E, 0.0).astype(BF)

    def head_means(xs):
        x = jnp.concatenate(xs, axis=0)
        high = x.astype(BF)
        low = (x - high.astype(F32)).astype(BF)
        means = nn(jnp.concatenate([high, low], axis=1), mean_of)
        return [means[i * T:(i + 1) * T] for i in range(len(xs))]

    def gather(near, enter, take, p):
        return (near[p].astype(F32) * take[0] + enter[p].astype(F32) * take[1]).astype(BF)

    small[1].wait()

    def normalize(c):
        forward[3](c).wait_recv()
        incopy(3, c).wait()
        for ps in groups(c, 4):
            cs = [gather(fnear, fenter, enter_f, p) for p in ps]
            for p, x in zip(ps, cs):
                carried[p] = x
            qbs = [q_ref[0, :, lanes(p)] * masks[2] for p in ps]
            atts = [att_s[p] + nn(qb, diag(x)) for p, qb, x in zip(ps, qbs, cs)]
            means = head_means([att * att for att in atts])
            invs = [lax.rsqrt(m + EPS) for m in means]
            normeds = each(lambda att, inv: att * inv, atts, invs)
            gains = [gain_ref[:, lanes(p)] for p in ps]
            for p, gain, normed in zip(ps, gains, normeds):
                out_ref[0, :, lanes(p)] = (gain * normed).astype(BF)
            dys = [dy_ref[0, :, lanes(p)].astype(F32) for p in ps]
            terms = each(lambda dy, normed: dy * normed, dys, normeds)
            for p, term in zip(ps, terms):
                gain_ctx[me, pl.ds(p, 1)] = jnp.sum(term, axis=0, keepdims=True)
            means = head_means(each(lambda term, gain: term * gain, terms, gains))
            gatts = [
                ((dy * gain - normed * m) * inv).astype(BF)
                for dy, gain, normed, m, inv in zip(dys, gains, normeds, means, invs)
            ]
            for p, gatt in zip(ps, gatts):
                gatt_s[p] = gatt
            full = each(tn, qbs, gatts)
            for p, x in zip(ps, full):
                back[p] = compact(x)
        backward[0](c).start()
        outcopy(0, c).start()

        @pl.when(c > 0)
        def _():
            combine_backward(c - 1)

    chunk_loop(normalize)

    def gcopy(d, slot):
        return pltpu.make_async_remote_copy(
            src_ref=gain_ctx.at[slot], dst_ref=gain_ctx.at[slot],
            send_sem=gsend.at[d - 1], recv_sem=grecv.at[d - 1],
            device_id={"ctx": lax.rem(me + d, n_ctx)},
        )

    def hcopy(d, slot):
        return pltpu.make_async_remote_copy(
            src_ref=gain_dp.at[slot], dst_ref=gain_dp.at[slot],
            send_sem=hsend.at[d - 1], recv_sem=hrecv.at[d - 1],
            device_id={"dp": lax.rem(mydp + d, n_dp)},
        )

    for d in range(1, n_ctx):
        gcopy(d, me).start()

    def gradients(c):
        for ps in groups(c, 4):
            gatts = [gatt_s[p] for p in ps]
            gss = each(stack, gatts)
            scores = [nt(gs, v_ref[0, :, lanes(p)]) for gs, p in zip(gss, ps)]
            for p, gs in zip(ps, gss):
                gv_s[p] = tn(weights[p], gs)
            gws = [x.astype(BF) * doc_mask[...] for x in scores]
            gqs = [
                nn(jnp.concatenate([gw[:T], gw[T:]], axis=1), stack(k_ref[0, :, lanes(p)]))
                + nt(gatt * masks[2], diag(carried[p]))
                for gw, gatt, p in zip(gws, gatts, ps)
            ]
            for p, gq in zip(ps, gqs):
                gq_ref[0, :, lanes(p)] = gq.astype(BF)
            for p, gw in zip(ps, gws):
                gk_s[p] = tn(gw, stack(q_ref[0, :, lanes(p)]))
        outcopy(1, c).start()
        exchange(c, combine_backward, relay_backward)

    chunk_loop(gradients)
    relay_backward(CHUNKS - 1)

    for d in range(1, n_ctx):
        gcopy(d, lax.rem(me - d + n_ctx, n_ctx)).wait_recv()
    total = gain_ctx[0]
    for i in range(1, n_ctx):
        total += gain_ctx[i]
    gain_dp[mydp] = total
    for d in range(1, n_dp):
        hcopy(d, mydp).start()

    def finish(c):
        backward[3](c).wait_recv()
        for ps in groups(c, 4):
            bds = [diag(gather(bnear, benter, enter_b, p)) for p in ps]
            after = masks[3]
            gks = [nt(v_ref[0, :, lanes(p)] * after, bd) for p, bd in zip(ps, bds)]
            gvs = [nn(k_ref[0, :, lanes(p)] * after, bd) for p, bd in zip(ps, bds)]
            for p, gk, gv in zip(ps, gks, gvs):
                gk_ref[0, :, lanes(p)] = (gk_s[p] + gk).astype(BF)
                gv_ref[0, :, lanes(p)] = (gv_s[p] + gv).astype(BF)
        outcopy(2, c).start()
        outcopy(3, c).start()

    chunk_loop(finish)

    for d in range(1, n_dp):
        hcopy(d, lax.rem(mydp - d + n_dp, n_dp)).wait_recv()
    total = gain_dp[0]
    for i in range(1, n_dp):
        total += gain_dp[i]
    gg_ref[...] = total * (1.0 / math.sqrt(total_tokens))
    gg_copy = pltpu.make_async_copy(gg_ref, gg_hbm, gg_sem)
    gg_copy.start()

    drain(forward)
    drain(backward)
    for d in range(1, n_ctx):
        gcopy(d, me).wait_send()
    for d in range(1, n_dp):
        hcopy(d, mydp).wait_send()
    for i in range(4):
        for c in range(CHUNKS):
            outcopy(i, c).wait()
    gg_copy.wait()


def write_out(*refs):
    sources, targets, held, in_sems, out_sems = refs[:5], refs[5:10], refs[10:15], refs[15], refs[16]

    def copies(from_refs, to_refs, sems):
        made = []
        for i, (source, target) in enumerate(zip(from_refs, to_refs)):
            if i == 4:
                made.append(pltpu.make_async_copy(source, target, sems.at[i, 0]))
                continue
            rows = source.shape[1] // 2
            for h in range(2):
                part = pl.ds(h * rows, rows)
                made.append(
                    pltpu.make_async_copy(source.at[:, part], target.at[:, part], sems.at[i, h])
                )
        return made

    loads, stores = copies(sources, held, in_sems), copies(held, targets, out_sems)
    for load in loads:
        load.start()
    for load, store in zip(loads, stores):
        load.wait()
        store.start()
    for store in stores:
        store.wait()


def per_device(queries, keys, values, grad_output, out_gain, doc_lengths):
    _, T, width = queries.shape
    n_ctx, n_dp = lax.axis_size("ctx"), lax.axis_size("dp")
    length = T * n_ctx
    longest = length // 3
    reach = min(n_ctx // 2 - 1, -(-(longest - 1) // (2 * T)))
    state = pltpu.VMEM((PAIRS, E, LANES), BF)
    far = pltpu.VMEM((reach, PAIRS, E, LANES), BF)
    hbm = pl.BlockSpec(memory_space=pltpu.HBM)
    data = jax.ShapeDtypeStruct((1, T, width), BF)
    dma = pltpu.SemaphoreType.DMA
    hops = [dma((CHUNKS,))] * 2 + [dma((reach, CHUNKS))] * 2 + [dma((CHUNKS,))] * 2
    shapes = (data,) * 4 + (jax.ShapeDtypeStruct((PAIRS, LANES), F32),)
    out = pl.pallas_call(
        functools.partial(kernel, n_ctx, n_dp, reach, n_dp * length),
        out_shape=shapes,
        in_specs=[hbm] * 6,
        out_specs=(hbm,) * 5,
        scratch_shapes=[
            pltpu.SMEM(doc_lengths.shape, jnp.int32),
            pltpu.VMEM((1, T, width), BF),
            pltpu.VMEM((1, T, width), BF),
            pltpu.VMEM((1, T, width), BF),
            pltpu.VMEM((1, T, width), BF),
            pltpu.VMEM((1, width), F32),
            dma((4, CHUNKS)),
            dma((2,)),
            pltpu.VMEM((1, T, width), BF),
            pltpu.VMEM((1, T, width), BF),
            pltpu.VMEM((1, T, width), BF),
            pltpu.VMEM((1, T, width), BF),
            pltpu.VMEM((PAIRS, LANES), F32),
            dma((4, CHUNKS)),
            dma,
            pltpu.VMEM((4, T, LANES), BF),
            pltpu.VMEM((2 * T, T), BF),
            state, state, state, state, state, state,
            far, far, state, state, state,
            pltpu.VMEM((PAIRS, 2 * T, T), BF),
            pltpu.VMEM((PAIRS, T, LANES), F32),
            pltpu.VMEM((PAIRS, T, LANES), BF),
            pltpu.VMEM((PAIRS, T, LANES), F32),
            pltpu.VMEM((PAIRS, T, LANES), F32),
            pltpu.VMEM((n_ctx, PAIRS, LANES), F32),
            pltpu.VMEM((n_dp, PAIRS, LANES), F32),
            hops, hops,
            dma((n_ctx - 1,)), dma((n_ctx - 1,)),
            dma((n_dp - 1,)), dma((n_dp - 1,)),
        ],
        compiler_params=pltpu.CompilerParams(
            collective_id=0, has_side_effects=True, vmem_limit_bytes=VMEM_LIMIT
        ),
    )(doc_lengths, queries, keys, values, grad_output, out_gain.reshape(1, width))
    out = pl.pallas_call(
        write_out,
        out_shape=shapes,
        in_specs=[hbm] * 5,
        out_specs=(hbm,) * 5,
        scratch_shapes=[pltpu.VMEM(x.shape, x.dtype) for x in shapes]
        + [dma((5, 2)), dma((5, 2))],
        compiler_params=pltpu.CompilerParams(vmem_limit_bytes=VMEM_LIMIT),
    )(*out)
    return (*out[:4], out[4].reshape(width))


def solution(mesh):
    seq = P("dp", "ctx", None)
    return jax.shard_map(
        per_device,
        mesh=mesh,
        in_specs=(seq, seq, seq, seq, P(), P("dp", None)),
        out_specs=(seq, seq, seq, seq, P()),
        check_vma=False,
    )
```

```python
import functools
import math

import jax
import jax.numpy as jnp
from jax import lax
from jax.experimental import pallas as pl
from jax.experimental.pallas import tpu as pltpu
from jax.sharding import PartitionSpec as P

H = 32
E = 64
LANES = 2 * E
PAIRS = H // 2
CHUNKS = 4
PER = PAIRS // CHUNKS
HALF = PER // 2
EPS = 1e-05
VMEM_LIMIT = 58 * 1024 * 1024
BF = jnp.bfloat16
F32 = jnp.float32


def nn(a, b):
    return lax.dot_general(a, b, (((1,), (0,)), ((), ())), preferred_element_type=F32)


def nt(a, b):
    return lax.dot_general(a, b, (((1,), (1,)), ((), ())), preferred_element_type=F32)


def tn(a, b):
    return lax.dot_general(a, b, (((0,), (0,)), ((), ())), preferred_element_type=F32)


def kernel(
    n_ctx, n_dp, reach, total_tokens,
    lengths_hbm, q_hbm, k_hbm, v_hbm, dy_hbm, gain_hbm,
    out_hbm, gq_hbm, gk_hbm, gv_hbm, gg_hbm,
    lengths_ref, q_ref, k_ref, v_ref, dy_ref, gain_ref, in_sem, small_sem,
    out_ref, gq_ref, gk_ref, gv_ref, gg_ref, out_sem, gg_sem,
    masks, doc_mask, own, back, fnear, bnear, fsum, bsum, fbuf, bbuf, fenter, benter, carried, weights, att_s, gatt_s, gk_s, gv_s,
    gain_ctx, gain_dp,
    fsems, bsems, gsend, grecv, hsend, hrecv, csend, crecv,
):
    me = lax.axis_index("ctx")
    chip, side = me // 2, lax.rem(me, 2)
    partner = me + 1 - 2 * side
    n_chips = n_ctx // 2
    mydp = lax.axis_index("dp")
    T = q_ref.shape[1]

    small = [
        pltpu.make_async_copy(lengths_hbm, lengths_ref, small_sem.at[0]),
        pltpu.make_async_copy(gain_hbm, gain_ref, small_sem.at[1]),
    ]

    def incopy(i, c):
        source, target = ((k_hbm, k_ref), (v_hbm, v_ref), (q_hbm, q_ref), (dy_hbm, dy_ref))[i]
        part = pl.ds(pl.multiple_of(c * (PER * LANES), PER * LANES), PER * LANES)
        return pltpu.make_async_copy(
            source.at[:, :, part], target.at[:, :, part], in_sem.at[i, c]
        )

    def outcopy(i, c):
        source, target = (
            (out_ref, out_hbm), (gq_ref, gq_hbm), (gk_ref, gk_hbm), (gv_ref, gv_hbm)
        )[i]
        part = pl.ds(pl.multiple_of(c * (PER * LANES), PER * LANES), PER * LANES)
        return pltpu.make_async_copy(
            source.at[:, :, part], target.at[:, :, part], out_sem.at[i, c]
        )

    small[0].start()
    for c in range(CHUNKS):
        incopy(0, c).start()
        incopy(1, c).start()
    for c in range(CHUNKS):
        incopy(2, c).start()
    small[1].start()
    for c in range(CHUNKS):
        incopy(3, c).start()

    barrier = pltpu.get_barrier_semaphore()
    for d in range(1, n_ctx):
        pl.semaphore_signal(barrier, inc=1, device_id={"ctx": lax.rem(me + d, n_ctx)})

    hub = n_ctx - 1

    @pl.when(me == hub)
    def _():
        for d in range(1, n_dp):
            pl.semaphore_signal(barrier, inc=1, device_id={"dp": lax.rem(mydp + d, n_dp)})


    small[0].wait()
    docs = lengths_ref.shape[1]
    offset = me * T
    first, last = jnp.int32(1 << 20), jnp.int32(-(1 << 20))
    hits_even, hits_odd = jnp.int32(0), jnp.int32(0)
    hits_f = [jnp.int32(0)] * (reach + 1)
    hits_b = [jnp.int32(0)] * (reach + 1)
    row = lax.broadcasted_iota(jnp.int32, (T, T), 0)
    col = lax.broadcasted_iota(jnp.int32, (T, T), 1)
    id_row = jnp.zeros((T, T), jnp.int32)
    id_col = jnp.zeros((T, T), jnp.int32)
    begin = -offset
    for i in range(docs):
        first = jnp.where(begin >= 0, jnp.minimum(first, begin), first)
        last = jnp.where(begin < T, jnp.maximum(last, begin), last)
        base = begin + side * T
        for d in range(2, reach + 1):
            hits_f[d] += jnp.where((base >= -(d - 1) * 2 * T) & (base < 0), 1, 0)
            hits_b[d] += jnp.where((base >= 2 * T) & (base < d * 2 * T), 1, 0)
        hits_even += jnp.where((base >= 0) & (base < T), 1, 0)
        hits_odd += jnp.where((base >= T) & (base < 2 * T), 1, 0)
        id_row += (row >= begin).astype(jnp.int32)
        id_col += (col >= begin).astype(jnp.int32)
        begin = begin + lengths_ref[0, i]
    coef_f = [jnp.where(hits_f[d] == 0, 1.0, 0.0).astype(F32) for d in range(reach + 1)]
    coef_b = [jnp.where(hits_b[d] == 0, 1.0, 0.0).astype(F32) for d in range(reach + 1)]
    keep_even = jnp.where(hits_even == 0, 1.0, 0.0).astype(F32)
    keep_odd = jnp.where(hits_odd == 0, 1.0, 0.0).astype(F32)
    odd = jnp.where(side == 1, 1.0, 0.0).astype(F32)
    sum_f = (odd + (1.0 - odd) * keep_odd, (1.0 - odd) + odd * keep_odd)
    sum_b = ((1.0 - odd) + odd * keep_even, odd + (1.0 - odd) * keep_even)
    enter_f = (odd, (1.0 - odd) + odd * keep_even)
    enter_b = (1.0 - odd, odd + (1.0 - odd) * keep_odd)
    dm = jnp.where((row >= col) & (id_row == id_col), 1.0, 0.0).astype(BF)
    doc_mask[0:T] = dm
    doc_mask[T:2 * T] = dm
    trow = lax.broadcasted_iota(jnp.int32, (T, LANES), 0)
    lane = lax.broadcasted_iota(jnp.int32, (T, LANES), 1)
    masks[0] = jnp.where(lane < E, 1.0, 0.0).astype(BF)
    masks[1] = jnp.where(lane < E, 0.0, 1.0).astype(BF)
    masks[2] = jnp.where(trow < first, 1.0, 0.0).astype(BF)
    masks[3] = jnp.where(trow >= last, 1.0, 0.0).astype(BF)

    for d in range(1, reach + 1):
        @pl.when(chip - d < 0)
        def _():
            fbuf[d - 1] = jnp.zeros(fbuf.shape[1:], BF)

        @pl.when(chip + d >= n_chips)
        def _():
            bbuf[d - 1] = jnp.zeros(bbuf.shape[1:], BF)

    def lanes(p):
        return pl.ds(pl.multiple_of(p * LANES, LANES), LANES)

    def compact(full):
        left = lax.broadcasted_iota(jnp.int32, (E, LANES), 1) < E
        return jnp.where(left, full[:E], full[E:]).astype(BF)

    def diag(c):
        return jnp.concatenate([c * masks[0, 0:E], c * masks[1, 0:E]], axis=0)

    def stack(x):
        return jnp.concatenate([x * masks[0], x * masks[1]], axis=0)

    def whole(c):
        return pl.ds(c * PER, PER)

    def mine(c):
        return pl.ds(c * PER + side * HALF, HALF)

    def links(state, near, summed, buf, enter, sems, sign):
        send, recv, far_send, far_recv, last_send, last_recv = sems

        def first_hop(c):
            return pltpu.make_async_remote_copy(
                src_ref=state.at[whole(c)], dst_ref=near.at[whole(c)],
                send_sem=send.at[c], recv_sem=recv.at[c], device_id={"ctx": partner},
            )

        def far_hop(d, c):
            return pltpu.make_async_remote_copy(
                src_ref=summed.at[mine(c)], dst_ref=buf.at[d - 1, mine(c)],
                send_sem=far_send.at[d - 1, c], recv_sem=far_recv.at[d - 1, c],
                device_id={"ctx": lax.rem(me + sign * 2 * d + n_ctx, n_ctx)},
            )

        def last_hop(c):
            return pltpu.make_async_remote_copy(
                src_ref=enter.at[mine(c)], dst_ref=enter.at[mine(c)],
                send_sem=last_send.at[c], recv_sem=last_recv.at[c],
                device_id={"ctx": partner},
            )

        def other_last_hop(c):
            theirs = pl.ds(c * PER + (1 - side) * HALF, HALF)
            return pltpu.make_async_remote_copy(
                src_ref=enter.at[theirs], dst_ref=enter.at[theirs],
                send_sem=last_send.at[c], recv_sem=last_recv.at[c],
                device_id={"ctx": partner},
            )

        def sends(d):
            return chip + d < n_chips if sign > 0 else chip - d >= 0

        def gets(d):
            return chip - d >= 0 if sign > 0 else chip + d < n_chips

        return first_hop, far_hop, last_hop, other_last_hop, sends, gets

    forward = links(own, fnear, fsum, fbuf, fenter, fsems, 1)
    backward = links(back, bnear, bsum, bbuf, benter, bsems, -1)

    def combine(c, link, state, near, summed, take):
        first_hop, far_hop, _, _, sends, _ = link
        first_hop(c).wait_recv()
        x = state[mine(c)].astype(F32) * take[0] + near[mine(c)].astype(F32) * take[1]
        summed[mine(c)] = x.astype(BF)
        for d in range(1, reach + 1):
            @pl.when(sends(d))
            def _():
                far_hop(d, c).start()

    def relay(c, link, buf, enter, coef):
        _, far_hop, last_hop, _, _, gets = link
        for d in range(1, reach + 1):
            @pl.when(gets(d))
            def _():
                far_hop(d, c).wait_recv()
        x = buf[0, mine(c)].astype(F32) * coef[1]
        for d in range(2, reach + 1):
            x += buf[d - 1, mine(c)].astype(F32) * coef[d]
        enter[mine(c)] = x.astype(BF)
        last_hop(c).start()

    def combine_forward(c):
        combine(c, forward, own, fnear, fsum, sum_f)

    def combine_backward(c):
        combine(c, backward, back, bnear, bsum, sum_b)

    def relay_forward(c):
        relay(c, forward, fbuf, fenter, coef_f)

    def relay_backward(c):
        relay(c, backward, bbuf, benter, coef_b)

    def exchange(c, combine_one, relay_one):
        @pl.when(c == 0)
        def _():
            combine_one(CHUNKS - 1)

        @pl.when(c > 0)
        def _():
            relay_one(c - 1)

    def drain(link):
        first_hop, far_hop, last_hop, _, sends, _ = link
        for c in range(CHUNKS):
            first_hop(c).wait_send()
            last_hop(c).wait_send()
            for d in range(1, reach + 1):
                @pl.when(sends(d))
                def _():
                    far_hop(d, c).wait_send()

    def each(f, *lists):
        return [f(*items) for items in zip(*lists)]

    def chunk_loop(body, low=0, high=CHUNKS):
        def step(c, _):
            body(c)
            return 0
        lax.fori_loop(low, high, step, 0)

    def groups(c, size):
        return [[c * PER + g + i for i in range(size)] for g in range(0, PER, size)]

    def states(c):
        incopy(0, c).wait()
        incopy(1, c).wait()
        for ps in groups(c, 4):
            ks = [k_ref[0, :, lanes(p)] * masks[3] for p in ps]
            full = [tn(k, v_ref[0, :, lanes(p)]) for k, p in zip(ks, ps)]
            for p, x in zip(ps, full):
                own[p] = compact(x)

        @pl.when(c == 0)
        def _():
            @pl.when(me == hub)
            def _():
                pl.semaphore_wait(barrier, n_ctx + n_dp - 2)

            @pl.when(me != hub)
            def _():
                pl.semaphore_wait(barrier, n_ctx - 1)

        forward[0](c).start()

        @pl.when(c > 0)
        def _():
            combine_forward(c - 1)

    chunk_loop(states)

    def inside(c):
        incopy(2, c).wait()
        for ps in groups(c, 4):
            qs = [stack(q_ref[0, :, lanes(p)]) for p in ps]
            scores = [nt(q, k_ref[0, :, lanes(p)]) for q, p in zip(qs, ps)]
            ws = [x.astype(BF) * doc_mask[...] for x in scores]
            for p, w in zip(ps, ws):
                weights[p] = w
            atts = [
                nn(jnp.concatenate([w[:T], w[T:]], axis=1), stack(v_ref[0, :, lanes(p)]))
                for w, p in zip(ws, ps)
            ]
            for p, att in zip(ps, atts):
                att_s[p] = att
        exchange(c, combine_forward, relay_forward)

    chunk_loop(inside)
    relay_forward(CHUNKS - 1)

    jrow = lax.broadcasted_iota(jnp.int32, (2 * LANES, LANES), 0)
    jlane = lax.broadcasted_iota(jnp.int32, (2 * LANES, LANES), 1)
    mean_of = jnp.where((lax.rem(jrow, LANES) < E) == (jlane < E), 1.0 / E, 0.0).astype(BF)

    def head_means(xs):
        x = jnp.concatenate(xs, axis=0)
        high = x.astype(BF)
        low = (x - high.astype(F32)).astype(BF)
        means = nn(jnp.concatenate([high, low], axis=1), mean_of)
        return [means[i * T:(i + 1) * T] for i in range(len(xs))]

    def gather(near, enter, take, p):
        return (near[p].astype(F32) * take[0] + enter[p].astype(F32) * take[1]).astype(BF)

    small[1].wait()

    def normalize(c):
        forward[3](c).wait_recv()
        incopy(3, c).wait()
        for ps in groups(c, 4):
            cs = [gather(fnear, fenter, enter_f, p) for p in ps]
            for p, x in zip(ps, cs):
                carried[p] = x
            qbs = [q_ref[0, :, lanes(p)] * masks[2] for p in ps]
            atts = [att_s[p] + nn(qb, diag(x)) for p, qb, x in zip(ps, qbs, cs)]
            means = head_means([att * att for att in atts])
            invs = [lax.rsqrt(m + EPS) for m in means]
            normeds = each(lambda att, inv: att * inv, atts, invs)
            gains = [gain_ref[:, lanes(p)] for p in ps]
            for p, gain, normed in zip(ps, gains, normeds):
                out_ref[0, :, lanes(p)] = (gain * normed).astype(BF)
            dys = [dy_ref[0, :, lanes(p)].astype(F32) for p in ps]
            terms = each(lambda dy, normed: dy * normed, dys, normeds)
            for p, term in zip(ps, terms):
                gain_ctx[me, pl.ds(p, 1)] = jnp.sum(term, axis=0, keepdims=True)
            means = head_means(each(lambda term, gain: term * gain, terms, gains))
            gatts = [
                ((dy * gain - normed * m) * inv).astype(BF)
                for dy, gain, normed, m, inv in zip(dys, gains, normeds, means, invs)
            ]
            for p, gatt in zip(ps, gatts):
                gatt_s[p] = gatt
            full = each(tn, qbs, gatts)
            for p, x in zip(ps, full):
                back[p] = compact(x)
        backward[0](c).start()
        outcopy(0, c).start()

        @pl.when(c > 0)
        def _():
            combine_backward(c - 1)

    chunk_loop(normalize)

    def gcopy(slot):
        return pltpu.make_async_remote_copy(
            src_ref=gain_ctx.at[slot], dst_ref=gain_ctx.at[slot],
            send_sem=gsend, recv_sem=grecv.at[slot], device_id={"ctx": hub},
        )

    def ccopy(i):
        return pltpu.make_async_remote_copy(
            src_ref=gg_ref, dst_ref=gg_ref,
            send_sem=csend.at[i], recv_sem=crecv, device_id={"ctx": i},
        )

    def hcopy(d, slot):
        return pltpu.make_async_remote_copy(
            src_ref=gain_dp.at[slot], dst_ref=gain_dp.at[slot],
            send_sem=hsend.at[d - 1], recv_sem=hrecv.at[d - 1],
            device_id={"dp": lax.rem(mydp + d, n_dp)},
        )

    @pl.when(me != hub)
    def _():
        gcopy(me).start()

    def sum_sequence():
        for i in range(n_ctx - 1):
            gcopy(i).wait_recv()
        total = gain_ctx[0]
        for i in range(1, n_ctx):
            total += gain_ctx[i]
        gain_dp[mydp] = total
        for d in range(1, n_dp):
            hcopy(d, mydp).start()

    def sum_all():
        for d in range(1, n_dp):
            hcopy(d, lax.rem(mydp - d + n_dp, n_dp)).wait_recv()
        total = gain_dp[0]
        for i in range(1, n_dp):
            total += gain_dp[i]
        gg_ref[...] = total * (1.0 / math.sqrt(total_tokens))
        for i in range(n_ctx - 1):
            ccopy(i).start()

    def gradients(c):
        @pl.when((me == hub) & (c == CHUNKS // 2))
        def _():
            sum_sequence()

        for ps in groups(c, 4):
            gatts = [gatt_s[p] for p in ps]
            gss = each(stack, gatts)
            scores = [nt(gs, v_ref[0, :, lanes(p)]) for gs, p in zip(gss, ps)]
            for p, gs in zip(ps, gss):
                gv_s[p] = tn(weights[p], gs)
            gws = [x.astype(BF) * doc_mask[...] for x in scores]
            gqs = [
                nn(jnp.concatenate([gw[:T], gw[T:]], axis=1), stack(k_ref[0, :, lanes(p)]))
                + nt(gatt * masks[2], diag(carried[p]))
                for gw, gatt, p in zip(gws, gatts, ps)
            ]
            for p, gq in zip(ps, gqs):
                gq_ref[0, :, lanes(p)] = gq.astype(BF)
            for p, gw in zip(ps, gws):
                gk_s[p] = tn(gw, stack(q_ref[0, :, lanes(p)]))
        outcopy(1, c).start()
        exchange(c, combine_backward, relay_backward)

    chunk_loop(gradients)
    relay_backward(CHUNKS - 1)

    def finish(c):
        @pl.when((me == hub) & (c == CHUNKS - 1))
        def _():
            sum_all()

        backward[3](c).wait_recv()
        for ps in groups(c, 4):
            bds = [diag(gather(bnear, benter, enter_b, p)) for p in ps]
            after = masks[3]
            gks = [nt(v_ref[0, :, lanes(p)] * after, bd) for p, bd in zip(ps, bds)]
            gvs = [nn(k_ref[0, :, lanes(p)] * after, bd) for p, bd in zip(ps, bds)]
            for p, gk, gv in zip(ps, gks, gvs):
                gk_ref[0, :, lanes(p)] = (gk_s[p] + gk).astype(BF)
                gv_ref[0, :, lanes(p)] = (gv_s[p] + gv).astype(BF)
        outcopy(2, c).start()
        outcopy(3, c).start()

    chunk_loop(finish)

    @pl.when(me != hub)
    def _():
        ccopy(0).wait_recv()

    gg_copy = pltpu.make_async_copy(gg_ref, gg_hbm, gg_sem)
    gg_copy.start()

    drain(forward)
    drain(backward)
    @pl.when(me != hub)
    def _():
        gcopy(me).wait_send()

    @pl.when(me == hub)
    def _():
        for d in range(1, n_dp):
            hcopy(d, mydp).wait_send()
        for i in range(n_ctx - 1):
            ccopy(i).wait_send()

    for i in range(4):
        for c in range(CHUNKS):
            outcopy(i, c).wait()
    gg_copy.wait()


def write_out(*refs):
    sources, targets, held, in_sems, out_sems = refs[:5], refs[5:10], refs[10:15], refs[15], refs[16]

    def copies(from_refs, to_refs, sems):
        made = []
        for i, (source, target) in enumerate(zip(from_refs, to_refs)):
            if i == 4:
                made.append(pltpu.make_async_copy(source, target, sems.at[i, 0]))
                continue
            rows = source.shape[1] // 2
            for h in range(2):
                part = pl.ds(h * rows, rows)
                made.append(
                    pltpu.make_async_copy(source.at[:, part], target.at[:, part], sems.at[i, h])
                )
        return made

    loads, stores = copies(sources, held, in_sems), copies(held, targets, out_sems)
    for load in loads:
        load.start()
    for load, store in zip(loads, stores):
        load.wait()
        store.start()
    for store in stores:
        store.wait()


def per_device(queries, keys, values, grad_output, out_gain, doc_lengths):
    _, T, width = queries.shape
    n_ctx, n_dp = lax.axis_size("ctx"), lax.axis_size("dp")
    length = T * n_ctx
    longest = length // 3
    reach = min(n_ctx // 2 - 1, -(-(longest - 1) // (2 * T)))
    state = pltpu.VMEM((PAIRS, E, LANES), BF)
    far = pltpu.VMEM((reach, PAIRS, E, LANES), BF)
    hbm = pl.BlockSpec(memory_space=pltpu.HBM)
    data = jax.ShapeDtypeStruct((1, T, width), BF)
    dma = pltpu.SemaphoreType.DMA
    hops = [dma((CHUNKS,))] * 2 + [dma((reach, CHUNKS))] * 2 + [dma((CHUNKS,))] * 2
    shapes = (data,) * 4 + (jax.ShapeDtypeStruct((PAIRS, LANES), F32),)
    out = pl.pallas_call(
        functools.partial(kernel, n_ctx, n_dp, reach, n_dp * length),
        out_shape=shapes,
        in_specs=[hbm] * 6,
        out_specs=(hbm,) * 5,
        scratch_shapes=[
            pltpu.SMEM(doc_lengths.shape, jnp.int32),
            pltpu.VMEM((1, T, width), BF),
            pltpu.VMEM((1, T, width), BF),
            pltpu.VMEM((1, T, width), BF),
            pltpu.VMEM((1, T, width), BF),
            pltpu.VMEM((1, width), F32),
            dma((4, CHUNKS)),
            dma((2,)),
            pltpu.VMEM((1, T, width), BF),
            pltpu.VMEM((1, T, width), BF),
            pltpu.VMEM((1, T, width), BF),
            pltpu.VMEM((1, T, width), BF),
            pltpu.VMEM((PAIRS, LANES), F32),
            dma((4, CHUNKS)),
            dma,
            pltpu.VMEM((4, T, LANES), BF),
            pltpu.VMEM((2 * T, T), BF),
            state, state, state, state, state, state,
            far, far, state, state, state,
            pltpu.VMEM((PAIRS, 2 * T, T), BF),
            pltpu.VMEM((PAIRS, T, LANES), F32),
            pltpu.VMEM((PAIRS, T, LANES), BF),
            pltpu.VMEM((PAIRS, T, LANES), F32),
            pltpu.VMEM((PAIRS, T, LANES), F32),
            pltpu.VMEM((n_ctx, PAIRS, LANES), F32),
            pltpu.VMEM((n_dp, PAIRS, LANES), F32),
            hops, hops,
            dma, dma((n_ctx - 1,)),
            dma((n_dp - 1,)), dma((n_dp - 1,)),
            dma((n_ctx - 1,)), dma,
        ],
        compiler_params=pltpu.CompilerParams(
            collective_id=0, has_side_effects=True, vmem_limit_bytes=VMEM_LIMIT
        ),
    )(doc_lengths, queries, keys, values, grad_output, out_gain.reshape(1, width))
    out = pl.pallas_call(
        write_out,
        out_shape=shapes,
        in_specs=[hbm] * 5,
        out_specs=(hbm,) * 5,
        scratch_shapes=[pltpu.VMEM(x.shape, x.dtype) for x in shapes]
        + [dma((5, 2)), dma((5, 2))],
        compiler_params=pltpu.CompilerParams(vmem_limit_bytes=VMEM_LIMIT),
    )(*out)
    return (*out[:4], out[4].reshape(width))


def solution(mesh):
    seq = P("dp", "ctx", None)
    return jax.shard_map(
        per_device,
        mesh=mesh,
        in_specs=(seq, seq, seq, seq, P(), P("dp", None)),
        out_specs=(seq, seq, seq, seq, P()),
        check_vma=False,
    )
```

```python
import functools
import math

import jax
import jax.numpy as jnp
from jax import lax
from jax.experimental import pallas as pl
from jax.experimental.pallas import tpu as pltpu
from jax.sharding import PartitionSpec as P

H = 32
E = 64
LANES = 2 * E
PAIRS = H // 2
CHUNKS = 4
PER = PAIRS // CHUNKS
HALF = PER // 2
EPS = 1e-05
VMEM_LIMIT = 58 * 1024 * 1024
BF = jnp.bfloat16
F32 = jnp.float32


def nn(a, b):
    return lax.dot_general(a, b, (((1,), (0,)), ((), ())), preferred_element_type=F32)


def nt(a, b):
    return lax.dot_general(a, b, (((1,), (1,)), ((), ())), preferred_element_type=F32)


def tn(a, b):
    return lax.dot_general(a, b, (((0,), (0,)), ((), ())), preferred_element_type=F32)


def kernel(
    n_ctx, n_dp, reach, total_tokens,
    lengths_hbm, q_hbm, k_hbm, v_hbm, dy_hbm, gain_hbm,
    out_hbm, gq_hbm, gk_hbm, gv_hbm, gg_hbm,
    lengths_ref, q_ref, k_ref, v_ref, dy_ref, gain_ref, in_sem, small_sem,
    out_ref, gq_ref, gk_ref, gv_ref, gg_ref, out_sem, gg_sem,
    masks, doc_mask, own, back, fnear, bnear, fsum, bsum, fbuf, bbuf, fenter, benter, carried, weights, att_s, gatt_s, gk_s, gv_s,
    gain_ctx, gain_dp,
    fsems, bsems, gsend, grecv, hsend, hrecv,
):
    me = lax.axis_index("ctx")
    chip, side = me // 2, lax.rem(me, 2)
    partner = me + 1 - 2 * side
    n_chips = n_ctx // 2
    mydp = lax.axis_index("dp")
    T = q_ref.shape[1]

    small = [
        pltpu.make_async_copy(lengths_hbm, lengths_ref, small_sem.at[0]),
        pltpu.make_async_copy(gain_hbm, gain_ref, small_sem.at[1]),
    ]

    def incopy(i, c):
        source, target = ((k_hbm, k_ref), (v_hbm, v_ref), (q_hbm, q_ref), (dy_hbm, dy_ref))[i]
        part = pl.ds(pl.multiple_of(c * (PER * LANES), PER * LANES), PER * LANES)
        return pltpu.make_async_copy(
            source.at[:, :, part], target.at[:, :, part], in_sem.at[i, c]
        )

    def outcopy(i, c):
        source, target = (
            (out_ref, out_hbm), (gq_ref, gq_hbm), (gk_ref, gk_hbm), (gv_ref, gv_hbm)
        )[i]
        part = pl.ds(pl.multiple_of(c * (PER * LANES), PER * LANES), PER * LANES)
        return pltpu.make_async_copy(
            source.at[:, :, part], target.at[:, :, part], out_sem.at[i, c]
        )

    small[0].start()
    for c in range(CHUNKS):
        incopy(0, c).start()
        incopy(1, c).start()
    for c in range(CHUNKS):
        incopy(2, c).start()
    small[1].start()
    for c in range(CHUNKS):
        incopy(3, c).start()

    barrier = pltpu.get_barrier_semaphore()
    for d in range(1, n_ctx):
        pl.semaphore_signal(barrier, inc=1, device_id={"ctx": lax.rem(me + d, n_ctx)})
    for d in range(1, n_dp):
        pl.semaphore_signal(barrier, inc=1, device_id={"dp": lax.rem(mydp + d, n_dp)})

    small[0].wait()
    docs = lengths_ref.shape[1]
    offset = me * T
    first, last = jnp.int32(1 << 20), jnp.int32(-(1 << 20))
    hits_even, hits_odd = jnp.int32(0), jnp.int32(0)
    hits_f = [jnp.int32(0)] * (reach + 1)
    hits_b = [jnp.int32(0)] * (reach + 1)
    row = lax.broadcasted_iota(jnp.int32, (T, T), 0)
    col = lax.broadcasted_iota(jnp.int32, (T, T), 1)
    id_row = jnp.zeros((T, T), jnp.int32)
    id_col = jnp.zeros((T, T), jnp.int32)
    begin = -offset
    for i in range(docs):
        first = jnp.where(begin >= 0, jnp.minimum(first, begin), first)
        last = jnp.where(begin < T, jnp.maximum(last, begin), last)
        base = begin + side * T
        for d in range(2, reach + 1):
            hits_f[d] += jnp.where((base >= -(d - 1) * 2 * T) & (base < 0), 1, 0)
            hits_b[d] += jnp.where((base >= 2 * T) & (base < d * 2 * T), 1, 0)
        hits_even += jnp.where((base >= 0) & (base < T), 1, 0)
        hits_odd += jnp.where((base >= T) & (base < 2 * T), 1, 0)
        id_row += (row >= begin).astype(jnp.int32)
        id_col += (col >= begin).astype(jnp.int32)
        begin = begin + lengths_ref[0, i]
    coef_f = [jnp.where(hits_f[d] == 0, 1.0, 0.0).astype(F32) for d in range(reach + 1)]
    coef_b = [jnp.where(hits_b[d] == 0, 1.0, 0.0).astype(F32) for d in range(reach + 1)]
    keep_even = jnp.where(hits_even == 0, 1.0, 0.0).astype(F32)
    keep_odd = jnp.where(hits_odd == 0, 1.0, 0.0).astype(F32)
    odd = jnp.where(side == 1, 1.0, 0.0).astype(F32)
    sum_f = (odd + (1.0 - odd) * keep_odd, (1.0 - odd) + odd * keep_odd)
    sum_b = ((1.0 - odd) + odd * keep_even, odd + (1.0 - odd) * keep_even)
    enter_f = (odd, (1.0 - odd) + odd * keep_even)
    enter_b = (1.0 - odd, odd + (1.0 - odd) * keep_odd)
    dm = jnp.where((row >= col) & (id_row == id_col), 1.0, 0.0).astype(BF)
    doc_mask[0:T] = dm
    doc_mask[T:2 * T] = dm
    trow = lax.broadcasted_iota(jnp.int32, (T, LANES), 0)
    lane = lax.broadcasted_iota(jnp.int32, (T, LANES), 1)
    masks[0] = jnp.where(lane < E, 1.0, 0.0).astype(BF)
    masks[1] = jnp.where(lane < E, 0.0, 1.0).astype(BF)
    masks[2] = jnp.where(trow < first, 1.0, 0.0).astype(BF)
    masks[3] = jnp.where(trow >= last, 1.0, 0.0).astype(BF)

    for d in range(1, reach + 1):
        @pl.when(chip - d < 0)
        def _():
            fbuf[d - 1] = jnp.zeros(fbuf.shape[1:], BF)

        @pl.when(chip + d >= n_chips)
        def _():
            bbuf[d - 1] = jnp.zeros(bbuf.shape[1:], BF)

    def lanes(p):
        return pl.ds(pl.multiple_of(p * LANES, LANES), LANES)

    def compact(full):
        left = lax.broadcasted_iota(jnp.int32, (E, LANES), 1) < E
        return jnp.where(left, full[:E], full[E:]).astype(BF)

    def diag(c):
        return jnp.concatenate([c * masks[0, 0:E], c * masks[1, 0:E]], axis=0)

    def stack(x):
        return jnp.concatenate([x * masks[0], x * masks[1]], axis=0)

    def whole(c):
        return pl.ds(c * PER, PER)

    def mine(c):
        return pl.ds(c * PER + side * HALF, HALF)

    def links(state, near, summed, buf, enter, sems, sign):
        send, recv, far_send, far_recv, last_send, last_recv = sems

        def first_hop(c):
            return pltpu.make_async_remote_copy(
                src_ref=state.at[whole(c)], dst_ref=near.at[whole(c)],
                send_sem=send.at[c], recv_sem=recv.at[c], device_id={"ctx": partner},
            )

        def far_hop(d, c):
            return pltpu.make_async_remote_copy(
                src_ref=summed.at[mine(c)], dst_ref=buf.at[d - 1, mine(c)],
                send_sem=far_send.at[d - 1, c], recv_sem=far_recv.at[d - 1, c],
                device_id={"ctx": lax.rem(me + sign * 2 * d + n_ctx, n_ctx)},
            )

        def last_hop(c):
            return pltpu.make_async_remote_copy(
                src_ref=enter.at[mine(c)], dst_ref=enter.at[mine(c)],
                send_sem=last_send.at[c], recv_sem=last_recv.at[c],
                device_id={"ctx": partner},
            )

        def other_last_hop(c):
            theirs = pl.ds(c * PER + (1 - side) * HALF, HALF)
            return pltpu.make_async_remote_copy(
                src_ref=enter.at[theirs], dst_ref=enter.at[theirs],
                send_sem=last_send.at[c], recv_sem=last_recv.at[c],
                device_id={"ctx": partner},
            )

        def sends(d):
            return chip + d < n_chips if sign > 0 else chip - d >= 0

        def gets(d):
            return chip - d >= 0 if sign > 0 else chip + d < n_chips

        return first_hop, far_hop, last_hop, other_last_hop, sends, gets

    forward = links(own, fnear, fsum, fbuf, fenter, fsems, 1)
    backward = links(back, bnear, bsum, bbuf, benter, bsems, -1)

    def combine(c, link, state, near, summed, take):
        first_hop, far_hop, _, _, sends, _ = link
        first_hop(c).wait_recv()
        x = state[mine(c)].astype(F32) * take[0] + near[mine(c)].astype(F32) * take[1]
        summed[mine(c)] = x.astype(BF)
        for d in range(1, reach + 1):
            @pl.when(sends(d))
            def _():
                far_hop(d, c).start()

    def relay(c, link, buf, enter, coef):
        _, far_hop, last_hop, _, _, gets = link
        for d in range(1, reach + 1):
            @pl.when(gets(d))
            def _():
                far_hop(d, c).wait_recv()
        x = buf[0, mine(c)].astype(F32) * coef[1]
        for d in range(2, reach + 1):
            x += buf[d - 1, mine(c)].astype(F32) * coef[d]
        enter[mine(c)] = x.astype(BF)
        last_hop(c).start()

    def combine_forward(c):
        combine(c, forward, own, fnear, fsum, sum_f)

    def combine_backward(c):
        combine(c, backward, back, bnear, bsum, sum_b)

    def relay_forward(c):
        relay(c, forward, fbuf, fenter, coef_f)

    def relay_backward(c):
        relay(c, backward, bbuf, benter, coef_b)

    def exchange(c, combine_one, relay_one):
        @pl.when(c == 0)
        def _():
            combine_one(CHUNKS - 1)

        @pl.when(c > 0)
        def _():
            relay_one(c - 1)

    def drain(link):
        first_hop, far_hop, last_hop, _, sends, _ = link
        for c in range(CHUNKS):
            first_hop(c).wait_send()
            last_hop(c).wait_send()
            for d in range(1, reach + 1):
                @pl.when(sends(d))
                def _():
                    far_hop(d, c).wait_send()

    def each(f, *lists):
        return [f(*items) for items in zip(*lists)]

    def chunk_loop(body, low=0, high=CHUNKS):
        def step(c, _):
            body(c)
            return 0
        lax.fori_loop(low, high, step, 0)

    def groups(c, size):
        return [[c * PER + g + i for i in range(size)] for g in range(0, PER, size)]

    def states(c):
        incopy(0, c).wait()
        incopy(1, c).wait()
        for ps in groups(c, 4):
            ks = [k_ref[0, :, lanes(p)] * masks[3] for p in ps]
            full = [tn(k, v_ref[0, :, lanes(p)]) for k, p in zip(ks, ps)]
            for p, x in zip(ps, full):
                own[p] = compact(x)

        @pl.when(c == 0)
        def _():
            pl.semaphore_wait(barrier, n_ctx + n_dp - 2)

        forward[0](c).start()

        @pl.when(c > 0)
        def _():
            combine_forward(c - 1)

    chunk_loop(states)

    def inside(c):
        incopy(2, c).wait()
        for ps in groups(c, 4):
            qs = [stack(q_ref[0, :, lanes(p)]) for p in ps]
            scores = [nt(q, k_ref[0, :, lanes(p)]) for q, p in zip(qs, ps)]
            ws = [x.astype(BF) * doc_mask[...] for x in scores]
            for p, w in zip(ps, ws):
                weights[p] = w
            atts = [
                nn(jnp.concatenate([w[:T], w[T:]], axis=1), stack(v_ref[0, :, lanes(p)]))
                for w, p in zip(ws, ps)
            ]
            for p, att in zip(ps, atts):
                att_s[p] = att
        exchange(c, combine_forward, relay_forward)

    chunk_loop(inside)
    relay_forward(CHUNKS - 1)

    jrow = lax.broadcasted_iota(jnp.int32, (2 * LANES, LANES), 0)
    jlane = lax.broadcasted_iota(jnp.int32, (2 * LANES, LANES), 1)
    mean_of = jnp.where((lax.rem(jrow, LANES) < E) == (jlane < E), 1.0 / E, 0.0).astype(BF)

    def head_means(xs):
        x = jnp.concatenate(xs, axis=0)
        high = x.astype(BF)
        low = (x - high.astype(F32)).astype(BF)
        means = nn(jnp.concatenate([high, low], axis=1), mean_of)
        return [means[i * T:(i + 1) * T] for i in range(len(xs))]

    def gather(near, enter, take, p):
        return (near[p].astype(F32) * take[0] + enter[p].astype(F32) * take[1]).astype(BF)

    small[1].wait()

    def normalize(c):
        forward[3](c).wait_recv()
        incopy(3, c).wait()
        for ps in groups(c, 4):
            cs = [gather(fnear, fenter, enter_f, p) for p in ps]
            for p, x in zip(ps, cs):
                carried[p] = x
            qbs = [q_ref[0, :, lanes(p)] * masks[2] for p in ps]
            atts = [att_s[p] + nn(qb, diag(x)) for p, qb, x in zip(ps, qbs, cs)]
            means = head_means([att * att for att in atts])
            invs = [lax.rsqrt(m + EPS) for m in means]
            normeds = each(lambda att, inv: att * inv, atts, invs)
            gains = [gain_ref[:, lanes(p)] for p in ps]
            for p, gain, normed in zip(ps, gains, normeds):
                out_ref[0, :, lanes(p)] = (gain * normed).astype(BF)
            dys = [dy_ref[0, :, lanes(p)].astype(F32) for p in ps]
            terms = each(lambda dy, normed: dy * normed, dys, normeds)
            for p, term in zip(ps, terms):
                gain_ctx[me, pl.ds(p, 1)] = jnp.sum(term, axis=0, keepdims=True)
            means = head_means(each(lambda term, gain: term * gain, terms, gains))
            gatts = [
                ((dy * gain - normed * m) * inv).astype(BF)
                for dy, gain, normed, m, inv in zip(dys, gains, normeds, means, invs)
            ]
            for p, gatt in zip(ps, gatts):
                gatt_s[p] = gatt
            full = each(tn, qbs, gatts)
            for p, x in zip(ps, full):
                back[p] = compact(x)
        backward[0](c).start()
        outcopy(0, c).start()

        @pl.when(c > 0)
        def _():
            combine_backward(c - 1)

    chunk_loop(normalize)

    def gcopy(d, slot):
        return pltpu.make_async_remote_copy(
            src_ref=gain_ctx.at[slot], dst_ref=gain_ctx.at[slot],
            send_sem=gsend.at[d - 1], recv_sem=grecv.at[d - 1],
            device_id={"ctx": lax.rem(me + d, n_ctx)},
        )

    def hcopy(d, slot):
        return pltpu.make_async_remote_copy(
            src_ref=gain_dp.at[slot], dst_ref=gain_dp.at[slot],
            send_sem=hsend.at[d - 1], recv_sem=hrecv.at[d - 1],
            device_id={"dp": lax.rem(mydp + d, n_dp)},
        )

    for d in range(1, n_ctx):
        gcopy(d, me).start()

    def sum_sequence():
        for d in range(1, n_ctx):
            gcopy(d, lax.rem(me - d + n_ctx, n_ctx)).wait_recv()
        total = gain_ctx[0]
        for i in range(1, n_ctx):
            total += gain_ctx[i]
        gain_dp[mydp] = total
        for d in range(1, n_dp):
            hcopy(d, mydp).start()

    def gradients(c):
        for ps in groups(c, 4):
            gatts = [gatt_s[p] for p in ps]
            gss = each(stack, gatts)
            scores = [nt(gs, v_ref[0, :, lanes(p)]) for gs, p in zip(gss, ps)]
            for p, gs in zip(ps, gss):
                gv_s[p] = tn(weights[p], gs)
            gws = [x.astype(BF) * doc_mask[...] for x in scores]
            gqs = [
                nn(jnp.concatenate([gw[:T], gw[T:]], axis=1), stack(k_ref[0, :, lanes(p)]))
                + nt(gatt * masks[2], diag(carried[p]))
                for gw, gatt, p in zip(gws, gatts, ps)
            ]
            for p, gq in zip(ps, gqs):
                gq_ref[0, :, lanes(p)] = gq.astype(BF)
            for p, gw in zip(ps, gws):
                gk_s[p] = tn(gw, stack(q_ref[0, :, lanes(p)]))
        outcopy(1, c).start()
        exchange(c, combine_backward, relay_backward)

        @pl.when(c == CHUNKS - 2)
        def _():
            sum_sequence()

    chunk_loop(gradients)
    relay_backward(CHUNKS - 1)

    def finish(c):
        backward[3](c).wait_recv()
        for ps in groups(c, 4):
            bds = [diag(gather(bnear, benter, enter_b, p)) for p in ps]
            after = masks[3]
            gks = [nt(v_ref[0, :, lanes(p)] * after, bd) for p, bd in zip(ps, bds)]
            gvs = [nn(k_ref[0, :, lanes(p)] * after, bd) for p, bd in zip(ps, bds)]
            for p, gk, gv in zip(ps, gks, gvs):
                gk_ref[0, :, lanes(p)] = (gk_s[p] + gk).astype(BF)
                gv_ref[0, :, lanes(p)] = (gv_s[p] + gv).astype(BF)
        outcopy(2, c).start()
        outcopy(3, c).start()

    chunk_loop(finish)

    for d in range(1, n_dp):
        hcopy(d, lax.rem(mydp - d + n_dp, n_dp)).wait_recv()
    total = gain_dp[0]
    for i in range(1, n_dp):
        total += gain_dp[i]
    gg_ref[...] = total * (1.0 / math.sqrt(total_tokens))
    gg_copy = pltpu.make_async_copy(gg_ref, gg_hbm, gg_sem)
    gg_copy.start()

    drain(forward)
    drain(backward)
    for d in range(1, n_ctx):
        gcopy(d, me).wait_send()
    for d in range(1, n_dp):
        hcopy(d, mydp).wait_send()
    for i in range(4):
        for c in range(CHUNKS):
            outcopy(i, c).wait()
    gg_copy.wait()


def write_out(*refs):
    sources, targets, held, in_sems, out_sems = refs[:5], refs[5:10], refs[10:15], refs[15], refs[16]

    def copies(from_refs, to_refs, sems):
        made = []
        for i, (source, target) in enumerate(zip(from_refs, to_refs)):
            if i == 4:
                made.append(pltpu.make_async_copy(source, target, sems.at[i, 0]))
                continue
            rows = source.shape[1] // 2
            for h in range(2):
                part = pl.ds(h * rows, rows)
                made.append(
                    pltpu.make_async_copy(source.at[:, part], target.at[:, part], sems.at[i, h])
                )
        return made

    loads, stores = copies(sources, held, in_sems), copies(held, targets, out_sems)
    for load in loads:
        load.start()
    for load, store in zip(loads, stores):
        load.wait()
        store.start()
    for store in stores:
        store.wait()


def per_device(queries, keys, values, grad_output, out_gain, doc_lengths):
    _, T, width = queries.shape
    n_ctx, n_dp = lax.axis_size("ctx"), lax.axis_size("dp")
    length = T * n_ctx
    longest = length // 3
    reach = min(n_ctx // 2 - 1, -(-(longest - 1) // (2 * T)))
    state = pltpu.VMEM((PAIRS, E, LANES), BF)
    far = pltpu.VMEM((reach, PAIRS, E, LANES), BF)
    hbm = pl.BlockSpec(memory_space=pltpu.HBM)
    data = jax.ShapeDtypeStruct((1, T, width), BF)
    dma = pltpu.SemaphoreType.DMA
    hops = [dma((CHUNKS,))] * 2 + [dma((reach, CHUNKS))] * 2 + [dma((CHUNKS,))] * 2
    shapes = (data,) * 4 + (jax.ShapeDtypeStruct((PAIRS, LANES), F32),)
    out = pl.pallas_call(
        functools.partial(kernel, n_ctx, n_dp, reach, n_dp * length),
        out_shape=shapes,
        in_specs=[hbm] * 6,
        out_specs=(hbm,) * 5,
        scratch_shapes=[
            pltpu.SMEM(doc_lengths.shape, jnp.int32),
            pltpu.VMEM((1, T, width), BF),
            pltpu.VMEM((1, T, width), BF),
            pltpu.VMEM((1, T, width), BF),
            pltpu.VMEM((1, T, width), BF),
            pltpu.VMEM((1, width), F32),
            dma((4, CHUNKS)),
            dma((2,)),
            pltpu.VMEM((1, T, width), BF),
            pltpu.VMEM((1, T, width), BF),
            pltpu.VMEM((1, T, width), BF),
            pltpu.VMEM((1, T, width), BF),
            pltpu.VMEM((PAIRS, LANES), F32),
            dma((4, CHUNKS)),
            dma,
            pltpu.VMEM((4, T, LANES), BF),
            pltpu.VMEM((2 * T, T), BF),
            state, state, state, state, state, state,
            far, far, state, state, state,
            pltpu.VMEM((PAIRS, 2 * T, T), BF),
            pltpu.VMEM((PAIRS, T, LANES), F32),
            pltpu.VMEM((PAIRS, T, LANES), BF),
            pltpu.VMEM((PAIRS, T, LANES), F32),
            pltpu.VMEM((PAIRS, T, LANES), F32),
            pltpu.VMEM((n_ctx, PAIRS, LANES), F32),
            pltpu.VMEM((n_dp, PAIRS, LANES), F32),
            hops, hops,
            dma((n_ctx - 1,)), dma((n_ctx - 1,)),
            dma((n_dp - 1,)), dma((n_dp - 1,)),
        ],
        compiler_params=pltpu.CompilerParams(
            collective_id=0, has_side_effects=True, vmem_limit_bytes=VMEM_LIMIT
        ),
    )(doc_lengths, queries, keys, values, grad_output, out_gain.reshape(1, width))
    out = pl.pallas_call(
        write_out,
        out_shape=shapes,
        in_specs=[hbm] * 5,
        out_specs=(hbm,) * 5,
        scratch_shapes=[pltpu.VMEM(x.shape, x.dtype) for x in shapes]
        + [dma((5, 2)), dma((5, 2))],
        compiler_params=pltpu.CompilerParams(vmem_limit_bytes=VMEM_LIMIT),
    )(*out)
    return (*out[:4], out[4].reshape(width))


def solution(mesh):
    seq = P("dp", "ctx", None)
    return jax.shard_map(
        per_device,
        mesh=mesh,
        in_specs=(seq, seq, seq, seq, P(), P("dp", None)),
        out_specs=(seq, seq, seq, seq, P()),
        check_vma=False,
    )
```
